32 devices in a mesh: lon: 8 (over z, y), lat: 4 (over x, core).
Axes of the slice: x: 2, y: 2, z: 4, core: 2. Of those that a mesh axis runs over, the one named last changes fastest.
Arguments:
- ocean_state: float32 [4, 16, 128, 1024], P(None, None, 'lat', 'lon'), may hold values from -4 to 4
- surface_state: float32 [3, 128, 1024], P(None, 'lat', 'lon'), may hold values from -3 to 3
- column_levels: int32 [128, 1024], P('lat', 'lon'), may hold values from 0 to 16
Outputs:
- ocean_next: float32 [4, 16, 128, 1024], P(None, None, 'lat', 'lon')
- surface_next: float32 [3, 128, 1024], P(None, 'lat', 'lon')
The draws below stay inside these ranges and needn't reach their ends.
Inputs may be any that keep to these rules, and one draw needn't show every extreme that they name: A column holds sea in the levels k < column_levels, counted from the surface; 0 marks land.
All inputs are finite; a program needn't handle non-finite values.
Results may differ from the reference program's by a relative error of at most 0.0003.
Values sent between devices are 32-bit elements; how exact they have to be, the bound alone decides.
A program may use at most 64 MiB of HBM per device.

```python
import math
import jax
import jax.numpy as jnp
from jax import lax

LEVELS = 16
NSUB = 4
NLAT = 128
NLON = 1024


def plant(values, own_key, smallest, largest):
    place = [jax.random.randint(jax.random.fold_in(own_key, axis), (), 0, length) for axis, length in enumerate(values.shape)]
    longest = values.shape.index(max(values.shape))
    neighbour = place[:longest] + [(place[longest] + 1) % values.shape[longest]] + place[longest + 1:]
    return values.at[tuple(place)].set(smallest).at[tuple(neighbour)].set(largest)


def block_scale(rng, dims, pieces, least, top_value):
    def one(position, parts):
        steps = jax.random.uniform(jax.random.fold_in(jax.random.fold_in(rng, 6), position), (parts,), jnp.float32, least / len(pieces), top_value / len(pieces))
        return jnp.repeat(jnp.exp(steps), dims[position] // parts).reshape((-1,) + (1,) * (len(dims) - position - 1))

    factor_of = one(*pieces[0])
    for cut in pieces[1:]:
        factor_of = factor_of * one(*cut)
    return factor_of


def gaussian(key, dims, spread, limit, pieces=(), held_as=jnp.bfloat16):
    values = spread * jax.random.normal(key, dims, jnp.float32)
    if pieces:
        values = values * block_scale(key, dims, pieces, -0.22, 0.18)
    return jnp.clip(values, -limit, limit).astype(held_as)


def setup_inputs(seed: int = 0) -> dict:
    seeds = jax.random.split(jax.random.key(seed), 4)
    return {
        "ocean_state": gaussian(seeds[0], (4, LEVELS, NLAT, NLON), 1.0, 4.0, ((2, 4), (3, 8)), jnp.float32),
        "surface_state": gaussian(seeds[1], (3, NLAT, NLON), 0.5, 3.0, ((1, 4), (2, 8)), jnp.float32),
        "column_levels": plant(jax.random.randint(seeds[2], (NLAT, NLON), 0, LEVELS + 1), jax.random.fold_in(seeds[2], 1), 0, LEVELS).astype(jnp.int32),
    }


epsilon = 1e-6
tracer_step = 0.1
surface_step = 1.2


def weno_pick(a, b, c, d, e):
    first_poly = (2.0 * a - 7.0 * b + 11.0 * c) / 6.0
    second_poly = (-b + 5.0 * c + 2.0 * d) / 6.0
    third_poly = (2.0 * c + 5.0 * d - e) / 6.0
    first_bend = a - 2.0 * b + c
    first_tilt = a - 4.0 * b + 3.0 * c
    middle_curvature = b - 2.0 * c + d
    second_tilt = b - d
    third_bend = c - 2.0 * d + e
    third_tilt = 3.0 * c - 4.0 * d + e
    first_smooth = epsilon + (13.0 / 12.0) * first_bend * first_bend + 0.25 * first_tilt * first_tilt
    second_smooth = epsilon + (13.0 / 12.0) * middle_curvature * middle_curvature + 0.25 * second_tilt * second_tilt
    third_smooth = epsilon + (13.0 / 12.0) * third_bend * third_bend + 0.25 * third_tilt * third_tilt
    leading_weight = 0.1 / (first_smooth * first_smooth)
    second_weight = 0.6 / (second_smooth * second_smooth)
    third_weight = 0.3 / (third_smooth * third_smooth)
    total_weight = leading_weight + second_weight + third_weight
    return (leading_weight * first_poly + second_weight * second_poly + third_weight * third_poly) / total_weight


def take_slab(source, offset, length, direction):
    return lax.slice_in_dim(source, offset, offset + length, axis=direction)


def flow_divergence(quantity, velocity, wet_mask, cell_count, direction):
    face_count = cell_count + 1
    a = take_slab(quantity, 0, face_count, direction)
    b = take_slab(quantity, 1, face_count, direction)
    c = take_slab(quantity, 2, face_count, direction)
    d = take_slab(quantity, 3, face_count, direction)
    e = take_slab(quantity, 4, face_count, direction)
    far_ahead = take_slab(quantity, 5, face_count, direction)
    left_value = weno_pick(a, b, c, d, e)
    eastern_reconstruction = weno_pick(far_ahead, e, d, c, b)
    face_speed = 0.5 * (take_slab(velocity, 2, face_count, direction) + take_slab(velocity, 3, face_count, direction))
    face_speed = face_speed * take_slab(wet_mask, 2, face_count, direction) * take_slab(wet_mask, 3, face_count, direction)
    face_flux = face_speed * jnp.where(face_speed >= 0.0, left_value, eastern_reconstruction)
    return take_slab(face_flux, 1, cell_count, direction) - take_slab(face_flux, 0, cell_count, direction)


def level_advection(quantities, wet_level):
    row_count = quantities.shape[1] - 6
    col_count = quantities.shape[2] - 6
    along_lon = flow_divergence(quantities[:, 3:-3, :], quantities[2:3, 3:-3, :], wet_level[None, 3:-3, :], col_count, 2)
    along_lat = flow_divergence(quantities[:, :, 3:-3], quantities[3:4, :, 3:-3], wet_level[None, :, 3:-3], row_count, 1)
    return along_lon + along_lat


def layer_step(gathered_arrays, ocean_layer_masks, advection, coriolis):
    levels = gathered_arrays.shape[1]
    thickness = 1.0 / levels
    theta_heat_tracer = gathered_arrays[0]
    haline_tracer = gathered_arrays[1]
    seawater_mass_per_volume = (-0.2 * theta_heat_tracer + 0.8 * haline_tracer - 0.05 * theta_heat_tracer * theta_heat_tracer
               + 0.03 * theta_heat_tracer * haline_tracer) * ocean_layer_masks
    pressure = thickness * (jnp.cumsum(seawater_mass_per_volume, axis=0) - 0.5 * seawater_mass_per_volume)
    grad_lon = 0.5 * (pressure[:, 3:-3, 4:-2] - pressure[:, 3:-3, 2:-4])
    grad_lat = 0.5 * (pressure[:, 4:-2, 3:-3] - pressure[:, 2:-4, 3:-3])
    interior = gathered_arrays[:, :, 3:-3, 3:-3]
    wet_mask = ocean_layer_masks[:, 3:-3, 3:-3]
    rotation = coriolis[None, :, None]
    accel_u = wet_mask * (-advection[2] + rotation * interior[3] - grad_lon)
    accel_v = wet_mask * (-advection[3] - rotation * interior[2] - grad_lat)
    new_temp = wet_mask * (interior[0] - tracer_step * advection[0])
    new_salt = wet_mask * (interior[1] - tracer_step * advection[1])
    u_star = wet_mask * interior[2] + tracer_step * accel_u
    v_star = wet_mask * interior[3] + tracer_step * accel_v
    depth_rim = thickness * jnp.sum(ocean_layer_masks[:, 1:-1, 1:-1], axis=0)
    safe_depth = jnp.maximum(depth_rim[2:-2, 2:-2], thickness)
    force_lon = thickness * jnp.sum(accel_u, axis=0) / safe_depth
    force_lat = thickness * jnp.sum(accel_v, axis=0) / safe_depth
    return new_temp, new_salt, u_star, v_star, force_lon, force_lat, depth_rim, safe_depth, wet_mask


def centered_lon(field):
    padded = jnp.pad(field, ((0, 0), (1, 1)))
    return 0.5 * (padded[:, 2:] - padded[:, :-2])


def centered_lat(field):
    padded = jnp.pad(field, ((1, 1), (0, 0)))
    return 0.5 * (padded[2:, :] - padded[:-2, :])


def substep_update(height, mean_u, mean_v, depth_rim, force_lon, force_lat):
    sea_mask = (depth_rim > 0.0).astype(depth_rim.dtype)
    height = sea_mask * (height - surface_step * (centered_lon(depth_rim * mean_u) + centered_lat(depth_rim * mean_v)))
    mean_u = sea_mask * (mean_u + surface_step * (force_lon - centered_lon(height)))
    mean_v = sea_mask * (mean_v + surface_step * (force_lat - centered_lat(height)))
    return height, mean_u, mean_v


def padded_globe(field, rim_width, signs):
    wide = jnp.concatenate([field[..., -rim_width:], field, field[..., :rim_width]], axis=-1)
    north = jnp.flip(wide[..., -rim_width:, :], axis=(-2, -1)) * signs
    return jnp.concatenate([jnp.zeros_like(north), wide, north], axis=-2)


def advect_level(level_pair):
    return level_advection(level_pair[0], level_pair[1])


def reference(ocean_state, surface_state, column_levels):
    thickness = 1.0 / LEVELS
    level_index = jnp.arange(LEVELS, dtype=jnp.int32)
    ocean_layer_masks = (level_index[:, None, None] < column_levels[None]).astype(ocean_state.dtype)
    field_signs = jnp.array([1.0, 1.0, -1.0, -1.0], dtype=ocean_state.dtype)[:, None, None, None]
    gathered_arrays = padded_globe(ocean_state, 3, field_signs)
    wet_rim = padded_globe(ocean_layer_masks, 3, 1.0)
    advection = jnp.moveaxis(lax.map(advect_level, (jnp.moveaxis(gathered_arrays, 1, 0), wet_rim)), 0, 1)
    latitude = (jnp.arange(NLAT, dtype=ocean_state.dtype) + 0.5) / NLAT
    coriolis = jnp.sin(math.pi * latitude - 0.5 * math.pi)
    new_temp, new_salt, u_star, v_star, force_lon, force_lat, depth_rim, safe_depth, wet_mask = layer_step(
        gathered_arrays, wet_rim, advection, coriolis)
    force_lon_rim = jnp.pad(force_lon, 2)
    force_lat_rim = jnp.pad(force_lat, 2)
    surface_signs = jnp.array([1.0, -1.0, -1.0], dtype=ocean_state.dtype)[:, None, None]
    height = surface_state[0]
    mean_u = surface_state[1]
    mean_v = surface_state[2]
    for substep in range(NSUB):
        rim_stack = padded_globe(jnp.stack([height, mean_u, mean_v]), 2, surface_signs)
        height, mean_u, mean_v = substep_update(rim_stack[0], rim_stack[1], rim_stack[2], depth_rim,
                                                force_lon_rim, force_lat_rim)
        height = height[2:-2, 2:-2]
        mean_u = mean_u[2:-2, 2:-2]
        mean_v = mean_v[2:-2, 2:-2]
    mean_star_u = thickness * jnp.sum(u_star, axis=0) / safe_depth
    mean_star_v = thickness * jnp.sum(v_star, axis=0) / safe_depth
    u_final = wet_mask * (u_star + mean_u - mean_star_u)
    v_final = wet_mask * (v_star + mean_v - mean_star_v)
    return (jnp.stack([new_temp, new_salt, u_final, v_final]), jnp.stack([height, mean_u, mean_v]))
```

```python
import functools
import math

import jax
import jax.numpy as jnp
from jax import lax
from jax.experimental import pallas as pl
from jax.experimental.pallas import tpu as pltpu
from jax.sharding import PartitionSpec as P

NSUB = 4
DEEP = 2 * NSUB
SUB = 8
epsilon = 1e-06
tracer_step = 0.1
surface_step = 1.2
f32 = jnp.float32


def face_flux(s, q0, q1, dm2, dm1, d0, dp1, dp2):
    pos = s >= 0.0
    c = jnp.where(pos, q0, q1)
    d1 = jnp.where(pos, dm2, dp2)
    d2 = jnp.where(pos, dm1, dp1)
    d3 = d0
    d4 = jnp.where(pos, dp1, dm1)
    k = 13.0 / 3.0
    b1 = d2 - d1
    b2 = d3 - d2
    b3 = d4 - d3
    t1 = 3.0 * d2 - d1
    t2 = d2 + d3
    t3 = d4 - 3.0 * d3
    s1 = (k * b1) * b1 + t1 * t1 + 4.0 * epsilon
    s2 = (k * b2) * b2 + t2 * t2 + 4.0 * epsilon
    s3 = (k * b3) * b3 + t3 * t3 + 4.0 * epsilon
    p23 = s2 * s3
    p13 = s1 * s3
    p12 = s1 * s2
    w1 = p23 * p23
    w2 = 6.0 * (p13 * p13)
    w3 = 3.0 * (p12 * p12)
    top = w1 * (2.0 * t1 - d2) + w2 * (t2 + d3) + w3 * (d3 - t3)
    total = 6.0 * (w1 + w2 + w3)
    r = pl.reciprocal(total, approx=True)
    r = r * (2.0 - total * r)
    return s * c + jnp.abs(s) * (top * r)


def left(x, n):
    return pltpu.roll(x, x.shape[-1] - n, axis=x.ndim - 1)


def right(x, n):
    return pltpu.roll(x, n, axis=x.ndim - 1)


def kernel(nx, ny, ocean, surface, levels_in, out, surf_out, ext, lon_own, lon_in, lat_out, lat_in, sa, sf,
           sa_lon, sf_lon, sa_north, sf_north, extra_lon, extra_lat, speed_lon, speed_lat, pbuf, fbuf,
           local_sem, send_sem, recv_sem):
    nlev, rows, cols = ocean.shape[1], ocean.shape[2], ocean.shape[3]
    top = SUB + rows
    full = top + SUB
    thickness = 1.0 / nlev
    wide = 8
    x = lax.axis_index("lon")
    y = lax.axis_index("lat")
    at_north = y == ny - 1
    east = {"lon": lax.rem(x + 1, nx), "lat": y}
    west = {"lon": lax.rem(x + nx - 1, nx), "lat": y}
    north = {"lon": jnp.where(at_north, nx - 1 - x, x), "lat": jnp.where(at_north, y, y + 1)}
    south = {"lon": x, "lat": jnp.maximum(y - 1, 0)}
    fold = jnp.where(at_north, 1, 0)
    far_row = pl.multiple_of(fold * top, SUB)

    load = pltpu.make_async_copy(ocean, ext.at[:, :, SUB:top, :], local_sem)
    load.start()

    sa[0:3, 0, SUB:top, :] = surface[...]
    sa[3, 0, SUB:top, :] = levels_in[...].astype(f32)

    @pl.when(y == 0)
    def _():
        sa[:, :, 0:SUB, :] = jnp.zeros((4, 2, SUB, cols), f32)
        sf[:, :, 0:SUB, :] = jnp.zeros((2, 2, SUB, cols), f32)
        lat_in[0] = jnp.zeros(lat_in.shape[1:], f32)

    barrier = pltpu.get_barrier_semaphore()
    for target in (east, west, north):
        pl.semaphore_signal(barrier, inc=1, device_id=target, device_id_type=pl.DeviceIdType.MESH)

    @pl.when(y > 0)
    def _():
        pl.semaphore_signal(barrier, inc=1, device_id=south, device_id_type=pl.DeviceIdType.MESH)

    pl.semaphore_wait(barrier, 3 + jnp.where(y > 0, 1, 0))

    def remote(src, dst, send, recv, target):
        return pltpu.make_async_remote_copy(
            src_ref=src, dst_ref=dst, send_sem=send_sem.at[send], recv_sem=recv_sem.at[recv],
            device_id=target, device_id_type=pl.DeviceIdType.MESH)

    class LonPair:
        def __init__(self, src, dst, base):
            self.go_east = remote(src, dst.at[0], base, base, east)
            self.go_west = remote(src, dst.at[1], base + 1, base + 1, west)

        def start(self):
            self.go_east.start()
            self.go_west.start()

        def wait_recv(self):
            self.go_east.wait_recv()
            self.go_west.wait_recv()

        def wait_send(self):
            self.go_east.wait_send()
            self.go_west.wait_send()

    class LatPair:
        def __init__(self, north_src, north_dst, south_src, dst_south, dst_north, base):
            self.go_north = remote(north_src, north_dst, base, base + fold, north)
            self.go_south = remote(south_src, dst_north, base + 1, base + 1, south)
            self.from_south = remote(north_src, dst_south, base, base, south)

        def start(self):
            self.go_north.start()

            @pl.when(y > 0)
            def _():
                self.go_south.start()

        def wait_recv(self):
            self.go_south.wait_recv()

            @pl.when(y > 0)
            def _():
                self.from_south.wait_recv()

        def wait_send(self):
            self.go_north.wait_send()

            @pl.when(y > 0)
            def _():
                self.go_south.wait_send()

    surf_lon = LonPair(sa.at[:, 0, SUB:top, :], sa_lon, 0)
    level_lon = LonPair(lon_own, lon_in, 2)
    force_lon_pair = LonPair(sf.at[:, 0, SUB:top, :], sf_lon, 4)
    level_lat = LatPair(lat_out.at[0], lat_in.at[fold], lat_out.at[1], lat_in.at[0], lat_in.at[1], 6)
    surf_lat = LatPair(sa_north, sa.at[:, :, pl.ds(far_row, SUB), :], sa.at[:, :, SUB:2 * SUB, :],
                       sa.at[:, :, 0:SUB, :], sa.at[:, :, top:full, :], 8)
    force_lat_pair = LatPair(sf_north, sf.at[:, :, pl.ds(far_row, SUB), :], sf.at[:, :, SUB:2 * SUB, :],
                             sf.at[:, :, 0:SUB, :], sf.at[:, :, top:full, :], 10)

    surf_lon.start()

    lane = lax.broadcasted_iota(jnp.int32, (rows, cols), 1)
    lane_full = lax.broadcasted_iota(jnp.int32, (full, cols), 1)
    spot = lane % wide
    owner = lane // wide
    sub8 = lax.broadcasted_iota(jnp.int32, (SUB, cols), 0)

    def mirrored(block):
        count = block.shape[0]
        a = lax.broadcasted_iota(jnp.int32, (cols, cols), 0)
        b = lax.broadcasted_iota(jnp.int32, (cols, cols), 1)
        flip_cols = (a + b == cols - 1).astype(f32)
        a = lax.broadcasted_iota(jnp.int32, (count, count), 0)
        b = lax.broadcasted_iota(jnp.int32, (count, count), 1)
        flip_rows = ((a // SUB == b // SUB) & (a % SUB + b % SUB == SUB - 1)).astype(f32)
        block = lax.dot(block, flip_cols, precision=lax.Precision.HIGHEST, preferred_element_type=f32)
        return lax.dot(flip_rows, block, precision=lax.Precision.HIGHEST, preferred_element_type=f32)

    load.wait()

    for q in range(4):
        pack = jnp.zeros((rows, cols), f32)
        for k in range(nlev):
            pack = jnp.where(owner == k, right(ext[q, k, SUB:top, :], wide * k + 3), pack)
        lon_own[q] = pack
    level_lon.start()

    half = nlev // 2
    for q in range(4):
        for h in range(half):
            n0 = ext[q, 2 * h, top - SUB:top, :]
            n1 = ext[q, 2 * h + 1, top - SUB:top, :]
            lat_out[0, q * half + h] = jnp.where(sub8 >= 4, n0, pltpu.roll(n1, 4, axis=0))
            s0 = ext[q, 2 * h, SUB:2 * SUB, :]
            s1 = ext[q, 2 * h + 1, SUB:2 * SUB, :]
            lat_out[1, q * half + h] = jnp.where(sub8 < 4, s0, pltpu.roll(s1, 4, axis=0))

    @pl.when(at_north)
    def _():
        for q in range(4):
            sign = 1.0 if q < 2 else -1.0
            block = lat_out[0, q * half:(q + 1) * half].reshape(half * SUB, cols)
            lat_out[0, q * half:(q + 1) * half] = (sign * mirrored(block)).reshape(half, SUB, cols)

    level_lat.start()

    def close_lon(fields, arrived, count):
        for f in range(count):
            fields[f, 1, SUB:top, :] = jnp.where(lane < cols // 2, arrived[1, f], arrived[0, f])

    def stage_north(fields, staged, signs):
        count = len(signs)
        for f in range(count):
            for part in range(2):
                staged[f, part] = fields[f, part, top - SUB:top, :]

        @pl.when(at_north)
        def _():
            for f in range(count):
                block = staged[f].reshape(2 * SUB, cols)
                staged[f] = (signs[f] * mirrored(block)).reshape(2, SUB, cols)

    surf_lon.wait_recv()
    close_lon(sa, sa_lon, 4)
    stage_north(sa, sa_north, (1.0, -1.0, -1.0, 1.0))
    surf_lat.start()

    level_lon.wait_recv()
    level_lat.wait_recv()
    surf_lat.wait_recv()

    for q in range(4):
        for h in range(half):
            for side, place in ((0, 0), (1, top)):
                block = lat_in[side, q * half + h]
                ext[q, 2 * h, place:place + SUB, :] = block
                ext[q, 2 * h + 1, place:place + SUB, :] = pltpu.roll(block, 4, axis=0)

    def lon_pack(q):
        return jnp.where(spot < 3, lon_in[0, q], lon_own[q])

    count_here = sa[3, 0, SUB:top, :]
    count_beside = sa[3, 1, SUB:top, :]
    level_of = owner.astype(f32)
    edge_wet = ((count_beside[:, cols - 1:cols] > level_of) & (count_here[:, 0:1] > level_of)).astype(f32)
    pack_u = lon_pack(2)
    edge_speed = 0.5 * (pack_u + left(pack_u, 1)) * edge_wet
    for q in range(4):
        pack = lon_pack(q)
        d = left(pack, 1) - pack
        extra_lon[q] = face_flux(edge_speed, pack, left(pack, 1), right(d, 2), right(d, 1), d, left(d, 1),
                                 left(d, 2))

    level_row = lax.broadcasted_iota(jnp.int32, (nlev, cols), 0).astype(f32)
    row_wet = ((sa[3, 0, SUB - 1:SUB, :] > level_row) & (sa[3, 0, SUB:SUB + 1, :] > level_row)).astype(f32)
    row_speed = 0.5 * (ext[3, :, SUB - 1, :] + ext[3, :, SUB, :]) * row_wet
    for q in range(4):
        cell = [ext[q, :, SUB - 3 + i, :] for i in range(6)]
        d = [cell[i + 1] - cell[i] for i in range(5)]
        extra_lat[q] = face_flux(row_speed, cell[2], cell[3], *d)

    def beside(q, k):
        both = jnp.where(spot < 3, lon_in[0, q], lon_in[1, q])
        return pltpu.roll(both, cols - 3 - wide * k, axis=1)

    def following(c, h):
        return left(jnp.where(lane == 0, h, c), 1)

    def advect(q, k, s_lon, s_lat):
        c = ext[q, k, SUB:top, :]
        h = beside(q, k)
        c1 = following(c, h)
        d = c1 - c
        dh = following(h, c) - h
        flux = face_flux(
            s_lon, c, c1,
            right(jnp.where(lane >= cols - 2, dh, d), 2),
            right(jnp.where(lane >= cols - 1, dh, d), 1),
            d,
            left(jnp.where(lane < 1, dh, d), 1),
            left(jnp.where(lane < 2, dh, d), 2))
        edge = pltpu.roll(extra_lon[q], cols - 2 - wide * k, axis=1)
        along = flux - jnp.where(lane == 0, edge, right(flux, 1))
        cell = [ext[q, k, SUB - 2 + i:top - 2 + i, :] for i in range(6)]
        d = [cell[i + 1] - cell[i] for i in range(5)]
        flux = face_flux(s_lat, cell[2], cell[3], *d)
        fbuf[SUB:top, :] = flux
        fbuf[SUB - 1:SUB, :] = extra_lat[q, pl.ds(k, 1), :]
        return along + (flux - fbuf[SUB - 1:top - 1, :])

    row = lax.broadcasted_iota(jnp.int32, (rows, cols), 0)
    latitude = ((y * rows + row).astype(f32) + 0.5) / float(ny * rows)
    coriolis = jnp.sin(math.pi * latitude - 0.5 * math.pi)

    def density(t, s, wet):
        return wet * (-0.2 * t + 0.8 * s - 0.05 * t * t + 0.03 * t * s)

    def momentum(k, carry):
        above, above_h, sum_u, sum_v, star_u, star_v = carry
        level = k.astype(f32)
        wet_full = (sa[3, 0] > level).astype(f32)
        wet = (sa[3, 0, SUB:top, :] > level).astype(f32)
        wet_h = (sa[3, 1, SUB:top, :] > level).astype(f32)
        wet_up = (sa[3, 0, SUB + 1:top + 1, :] > level).astype(f32)
        rho = density(ext[0, k], ext[1, k], wet_full)
        above = above + rho
        pressure = thickness * (above - 0.5 * rho)
        rho_h = density(beside(0, k), beside(1, k), wet_h)
        above_h = above_h + rho_h
        pressure_h = thickness * (above_h - 0.5 * rho_h)
        pbuf[...] = pressure
        p = pbuf[SUB:top, :]
        grad_lon = 0.5 * (following(p, pressure_h) - right(jnp.where(lane == cols - 1, pressure_h, p), 1))
        grad_lat = 0.5 * (pbuf[SUB + 1:top + 1, :] - pbuf[SUB - 1:top - 1, :])
        u = ext[2, k, SUB:top, :]
        v = ext[3, k, SUB:top, :]
        s_lon = 0.5 * (u + following(u, beside(2, k))) * wet * following(wet, wet_h)
        s_lat = 0.5 * (v + ext[3, k, SUB + 1:top + 1, :]) * wet * wet_up
        speed_lon[k] = s_lon
        speed_lat[k] = s_lat
        accel_u = wet * (coriolis * v - advect(2, k, s_lon, s_lat) - grad_lon)
        accel_v = wet * (-advect(3, k, s_lon, s_lat) - coriolis * u - grad_lat)
        u_star = wet * u + tracer_step * accel_u
        v_star = wet * v + tracer_step * accel_v
        out[2, k] = u_star
        out[3, k] = v_star
        return above, above_h, sum_u + accel_u, sum_v + accel_v, star_u + u_star, star_v + v_star

    zero = jnp.zeros((rows, cols), f32)
    _, _, sum_u, sum_v, star_u, star_v = lax.fori_loop(
        0, nlev, momentum, (jnp.zeros((full, cols), f32), zero, zero, zero, zero, zero))
    per_depth = thickness / jnp.maximum(thickness * sa[3, 0, SUB:top, :], thickness)
    sf[0, 0, SUB:top, :] = sum_u * per_depth
    sf[1, 0, SUB:top, :] = sum_v * per_depth
    mean_star_u = star_u * per_depth
    mean_star_v = star_v * per_depth
    force_lon_pair.start()

    def tracers(k, carry):
        wet = (sa[3, 0, SUB:top, :] > k.astype(f32)).astype(f32)
        s_lon = speed_lon[k]
        s_lat = speed_lat[k]
        for q in range(2):
            out[q, k] = wet * (ext[q, k, SUB:top, :] - tracer_step * advect(q, k, s_lon, s_lat))
        return carry

    lax.fori_loop(0, nlev // 2, tracers, 0)
    force_lon_pair.wait_recv()
    close_lon(sf, sf_lon, 2)
    stage_north(sf, sf_north, (-1.0, -1.0))
    force_lat_pair.start()
    lax.fori_loop(nlev // 2, nlev, tracers, 0)
    force_lat_pair.wait_recv()

    def slope_lon(c, h):
        up_c = left(jnp.where(lane_full == 0, h, c), 1)
        up_h = left(jnp.where(lane_full == 0, c, h), 1)
        down_c = right(jnp.where(lane_full == cols - 1, h, c), 1)
        down_h = right(jnp.where(lane_full == cols - 1, c, h), 1)
        return 0.5 * (up_c - down_c), 0.5 * (up_h - down_h)

    def slope_lat(c, h):
        return tuple(0.5 * (pltpu.roll(a, full - 1, axis=0) - pltpu.roll(a, 1, axis=0)) for a in (c, h))

    both = (0, 1)
    height = [sa[0, i] for i in both]
    mean_u = [sa[1, i] for i in both]
    mean_v = [sa[2, i] for i in both]
    depth = [thickness * sa[3, i] for i in both]
    sea = [(sa[3, i] > 0.0).astype(f32) for i in both]
    for _ in range(NSUB):
        dx = slope_lon(*[depth[i] * mean_u[i] for i in both])
        dy = slope_lat(*[depth[i] * mean_v[i] for i in both])
        height = [sea[i] * (height[i] - surface_step * (dx[i] + dy[i])) for i in both]
        dx = slope_lon(*height)
        dy = slope_lat(*height)
        mean_u = [sea[i] * (mean_u[i] + surface_step * (sf[0, i] - dx[i])) for i in both]
        mean_v = [sea[i] * (mean_v[i] + surface_step * (sf[1, i] - dy[i])) for i in both]
    surf_out[0] = height[0][SUB:top]
    surf_out[1] = mean_u[0][SUB:top]
    surf_out[2] = mean_v[0][SUB:top]
    gain_u = mean_u[0][SUB:top] - mean_star_u
    gain_v = mean_v[0][SUB:top] - mean_star_v

    def finish(k, carry):
        wet = (sa[3, 0, SUB:top, :] > k.astype(f32)).astype(f32)
        out[2, k] = wet * (out[2, k] + gain_u)
        out[3, k] = wet * (out[3, k] + gain_v)
        return carry

    lax.fori_loop(0, nlev, finish, 0)

    for pair in (surf_lon, level_lon, level_lat, surf_lat, force_lon_pair, force_lat_pair):
        pair.wait_send()


def on_device(nx, ny, ocean_state, surface_state, column_levels):
    _, nlev, rows, cols = ocean_state.shape
    if cols % 128 or nlev * 8 > cols or nlev % 2 or rows % SUB or DEEP > SUB or nx % 2:
        raise ValueError("tile shape")
    full = rows + 2 * SUB
    vmem = pltpu.VMEM
    return pl.pallas_call(
        functools.partial(kernel, nx, ny),
        out_shape=(jax.ShapeDtypeStruct(ocean_state.shape, f32), jax.ShapeDtypeStruct(surface_state.shape, f32)),
        in_specs=[pl.BlockSpec(memory_space=pl.ANY), pl.BlockSpec(memory_space=vmem), pl.BlockSpec(memory_space=vmem)],
        out_specs=(pl.BlockSpec(memory_space=vmem), pl.BlockSpec(memory_space=vmem)),
        scratch_shapes=[
            vmem((4, nlev, full, cols), f32),
            vmem((4, rows, cols), f32),
            vmem((2, 4, rows, cols), f32),
            vmem((2, 2 * nlev, SUB, cols), f32),
            vmem((2, 2 * nlev, SUB, cols), f32),
            vmem((4, 2, full, cols), f32),
            vmem((2, 2, full, cols), f32),
            vmem((2, 4, rows, cols), f32),
            vmem((2, 2, rows, cols), f32),
            vmem((4, 2, SUB, cols), f32),
            vmem((2, 2, SUB, cols), f32),
            vmem((4, rows, cols), f32),
            vmem((4, nlev, cols), f32),
            vmem((nlev, rows, cols), f32),
            vmem((nlev, rows, cols), f32),
            vmem((full, cols), f32),
            vmem((full, cols), f32),
            pltpu.SemaphoreType.DMA,
            pltpu.SemaphoreType.DMA((12,)),
            pltpu.SemaphoreType.DMA((12,)),
        ],
        compiler_params=pltpu.CompilerParams(collective_id=0, has_side_effects=True,
                                             vmem_limit_bytes=32 * 1024 * 1024),
    )(ocean_state, surface_state, column_levels)


def solution(mesh):
    return jax.shard_map(
        functools.partial(on_device, mesh.shape["lon"], mesh.shape["lat"]),
        mesh=mesh,
        in_specs=(P(None, None, "lat", "lon"), P(None, "lat", "lon"), P("lat", "lon")),
        out_specs=(P(None, None, "lat", "lon"), P(None, "lat", "lon")),
        check_vma=False,
    )
```

```python
import functools
import math

import jax
import jax.numpy as jnp
from jax import lax
from jax.experimental import pallas as pl
from jax.experimental.pallas import tpu as pltpu
from jax.sharding import PartitionSpec as P

NSUB = 4
DEEP = 2 * NSUB
SUB = 8
epsilon = 1e-06
tracer_step = 0.1
surface_step = 1.2
f32 = jnp.float32


def face_flux(s, q0, q1, dm2, dm1, d0, dp1, dp2):
    pos = s >= 0.0
    sixth = jnp.abs(s) * (1.0 / 6.0)
    c = jnp.where(pos, q0, q1)
    d1 = jnp.where(pos, dm2, dp2)
    d2 = jnp.where(pos, dm1, dp1)
    d3 = d0
    d4 = jnp.where(pos, dp1, dm1)
    k = 13.0 / 3.0
    b1 = d2 - d1
    b2 = d3 - d2
    b3 = d4 - d3
    t1 = 3.0 * d2 - d1
    t2 = d2 + d3
    t3 = d4 - 3.0 * d3
    s1 = (k * b1) * b1 + t1 * t1 + 4.0 * epsilon
    s2 = (k * b2) * b2 + t2 * t2 + 4.0 * epsilon
    s3 = (k * b3) * b3 + t3 * t3 + 4.0 * epsilon
    p23 = s2 * s3
    p13 = s1 * s3
    p12 = s1 * s2
    w1 = p23 * p23
    w2 = 6.0 * (p13 * p13)
    w3 = 3.0 * (p12 * p12)
    top = w1 * (2.0 * t1 - d2) + w2 * (t2 + d3) + w3 * (d3 - t3)
    return s * c + sixth * (top * pl.reciprocal(w1 + w2 + w3, approx=True))


def left(x, n):
    return pltpu.roll(x, x.shape[-1] - n, axis=x.ndim - 1)


def right(x, n):
    return pltpu.roll(x, n, axis=x.ndim - 1)


def kernel(nx, ny, ocean, surface, levels_in, out_hbm, surf_out, ext, lon_own, lon_in, lat_out, lat_in, sa, sf,
           sa_lon, sf_lon, sa_north, sf_north, extra_lon, extra_lat, speed_lon, speed_lat, pbuf, fbuf,
           flat, out, counts, local_sem, store_sem, send_sem, recv_sem):
    nlev, rows, cols = ocean.shape[1], ocean.shape[2], ocean.shape[3]
    top = SUB + rows
    full = top + SUB
    thickness = 1.0 / nlev
    wide = 8
    x = lax.axis_index("lon")
    y = lax.axis_index("lat")
    at_north = y == ny - 1
    east = {"lon": lax.rem(x + 1, nx), "lat": y}
    west = {"lon": lax.rem(x + nx - 1, nx), "lat": y}
    north = {"lon": jnp.where(at_north, nx - 1 - x, x), "lat": jnp.where(at_north, y, y + 1)}
    south = {"lon": x, "lat": jnp.maximum(y - 1, 0)}
    fold = jnp.where(at_north, 1, 0)
    far_row = pl.multiple_of(fold * top, SUB)

    load = pltpu.make_async_copy(ocean, ext.at[:, :, SUB:top, :], local_sem.at[0])
    load_surface = pltpu.make_async_copy(surface, sa.at[0:3, 0, SUB:top, :], local_sem.at[1])
    load_counts = pltpu.make_async_copy(levels_in, counts, local_sem.at[2])
    load.start()
    load_surface.start()
    load_counts.start()

    @pl.when(y == 0)
    def _():
        sa[:, :, 0:SUB, :] = jnp.zeros((4, 2, SUB, cols), f32)
        sf[:, :, 0:SUB, :] = jnp.zeros((2, 2, SUB, cols), f32)
        lat_in[0] = jnp.zeros(lat_in.shape[1:], f32)

    barrier = pltpu.get_barrier_semaphore()
    for target in (east, west, north):
        pl.semaphore_signal(barrier, inc=1, device_id=target, device_id_type=pl.DeviceIdType.MESH)

    @pl.when(y > 0)
    def _():
        pl.semaphore_signal(barrier, inc=1, device_id=south, device_id_type=pl.DeviceIdType.MESH)

    def remote(src, dst, send, recv, target):
        return pltpu.make_async_remote_copy(
            src_ref=src, dst_ref=dst, send_sem=send_sem.at[send], recv_sem=recv_sem.at[recv],
            device_id=target, device_id_type=pl.DeviceIdType.MESH)

    class LonPair:
        def __init__(self, src, dst, base):
            self.go_east = remote(src, dst.at[0], base, base, east)
            self.go_west = remote(src, dst.at[1], base + 1, base + 1, west)

        def start(self):
            self.go_east.start()
            self.go_west.start()

        def wait_recv(self):
            self.go_east.wait_recv()
            self.go_west.wait_recv()

        def wait_send(self):
            self.go_east.wait_send()
            self.go_west.wait_send()

    class LatPair:
        def __init__(self, north_src, north_dst, south_src, dst_south, dst_north, base):
            self.go_north = remote(north_src, north_dst, base, base + fold, north)
            self.go_south = remote(south_src, dst_north, base + 1, base + 1, south)
            self.from_south = remote(north_src, dst_south, base, base, south)

        def start(self):
            self.go_north.start()

            @pl.when(y > 0)
            def _():
                self.go_south.start()

        def wait_recv(self):
            self.go_south.wait_recv()

            @pl.when(y > 0)
            def _():
                self.from_south.wait_recv()

        def wait_send(self):
            self.go_north.wait_send()

            @pl.when(y > 0)
            def _():
                self.go_south.wait_send()

    surf_lon = LonPair(sa.at[:, 0, SUB:top, :], sa_lon, 0)
    level_lon = LonPair(lon_own, lon_in, 2)
    force_lon_pair = LonPair(sf.at[:, 0, SUB:top, :], sf_lon, 4)
    level_lat = LatPair(lat_out.at[0], lat_in.at[fold], lat_out.at[1], lat_in.at[0], lat_in.at[1], 6)
    surf_lat = LatPair(sa_north, sa.at[:, :, pl.ds(far_row, SUB), :], sa.at[:, :, SUB:2 * SUB, :],
                       sa.at[:, :, 0:SUB, :], sa.at[:, :, top:full, :], 8)
    force_lat_pair = LatPair(sf_north, sf.at[:, :, pl.ds(far_row, SUB), :], sf.at[:, :, SUB:2 * SUB, :],
                             sf.at[:, :, 0:SUB, :], sf.at[:, :, top:full, :], 10)

    lane = lax.broadcasted_iota(jnp.int32, (rows, cols), 1)
    lane_full = lax.broadcasted_iota(jnp.int32, (full, cols), 1)
    spot = lane % wide
    owner = lane // wide
    sub8 = lax.broadcasted_iota(jnp.int32, (SUB, cols), 0)

    def mirrored(block):
        count = block.shape[0]
        a = lax.broadcasted_iota(jnp.int32, (cols, cols), 0)
        b = lax.broadcasted_iota(jnp.int32, (cols, cols), 1)
        flip_cols = (a + b == cols - 1).astype(f32)
        a = lax.broadcasted_iota(jnp.int32, (count, count), 0)
        b = lax.broadcasted_iota(jnp.int32, (count, count), 1)
        flip_rows = ((a // SUB == b // SUB) & (a % SUB + b % SUB == SUB - 1)).astype(f32)
        block = lax.dot(block, flip_cols, precision=lax.Precision.HIGHEST, preferred_element_type=f32)
        return lax.dot(flip_rows, block, precision=lax.Precision.HIGHEST, preferred_element_type=f32)

    load.wait()
    half = nlev // 2
    for q in range(4):
        for h in range(half):
            n0 = ext[q, 2 * h, top - SUB:top, :]
            n1 = ext[q, 2 * h + 1, top - SUB:top, :]
            lat_out[0, q * half + h] = jnp.where(sub8 >= 4, n0, pltpu.roll(n1, 4, axis=0))
            s0 = ext[q, 2 * h, SUB:2 * SUB, :]
            s1 = ext[q, 2 * h + 1, SUB:2 * SUB, :]
            lat_out[1, q * half + h] = jnp.where(sub8 < 4, s0, pltpu.roll(s1, 4, axis=0))

    @pl.when(at_north)
    def _():
        for q in range(4):
            sign = 1.0 if q < 2 else -1.0
            block = lat_out[0, q * half:(q + 1) * half].reshape(half * SUB, cols)
            lat_out[0, q * half:(q + 1) * half] = (sign * mirrored(block)).reshape(half, SUB, cols)

    load_surface.wait()
    load_counts.wait()
    sa[3, 0, SUB:top, :] = counts[...].astype(f32)
    pl.semaphore_wait(barrier, 3 + jnp.where(y > 0, 1, 0))
    surf_lon.start()
    level_lat.start()

    for q in range(4):
        pack = jnp.zeros((rows, cols), f32)
        for k in range(nlev):
            pack = jnp.where(owner == k, right(ext[q, k, SUB:top, :], wide * k + 3), pack)
        lon_own[q] = pack
    level_lon.start()

    def close_lon(fields, arrived, count):
        for f in range(count):
            fields[f, 1, SUB:top, :] = jnp.where(lane < cols // 2, arrived[1, f], arrived[0, f])

    def stage_north(fields, staged, signs):
        count = len(signs)
        for f in range(count):
            for part in range(2):
                staged[f, part] = fields[f, part, top - SUB:top, :]

        @pl.when(at_north)
        def _():
            for f in range(count):
                block = staged[f].reshape(2 * SUB, cols)
                staged[f] = (signs[f] * mirrored(block)).reshape(2, SUB, cols)

    surf_lon.wait_recv()
    close_lon(sa, sa_lon, 4)
    stage_north(sa, sa_north, (1.0, -1.0, -1.0, 1.0))
    surf_lat.start()

    def face_rows(q, k, s, first, count):
        cell = [ext[q, k, first - 2 + i:first - 2 + i + count, :] for i in range(6)]
        return face_flux(s, cell[2], cell[3], *[cell[i + 1] - cell[i] for i in range(5)])

    def lat_speed(k, first, count):
        level = k.astype(f32)
        wet = (sa[3, 0, first:first + count, :] > level).astype(f32)
        wet_up = (sa[3, 0, first + 1:first + 1 + count, :] > level).astype(f32)
        return 0.5 * (ext[3, k, first:first + count, :] + ext[3, k, first + 1:first + 1 + count, :]) * wet * wet_up

    inner, inner_count = 2 * SUB, rows - 2 * SUB

    def inner_faces(i, carry):
        for k in (2 * i, 2 * i + 1):
            s = lat_speed(k, inner, inner_count)
            for q in range(4):
                flat[q, k] = face_rows(q, k, s, inner, inner_count)
        return carry

    lax.fori_loop(0, half, inner_faces, 0)

    level_lon.wait_recv()
    level_lat.wait_recv()
    surf_lat.wait_recv()

    for q in range(4):
        for h in range(half):
            for side, place in ((0, 0), (1, top)):
                block = lat_in[side, q * half + h]
                ext[q, 2 * h, place:place + SUB, :] = block
                ext[q, 2 * h + 1, place:place + SUB, :] = pltpu.roll(block, 4, axis=0)

    def lon_pack(q):
        return jnp.where(spot < 3, lon_in[0, q], lon_own[q])

    count_here = sa[3, 0, SUB:top, :]
    count_beside = sa[3, 1, SUB:top, :]
    level_of = owner.astype(f32)
    edge_wet = ((count_beside[:, cols - 1:cols] > level_of) & (count_here[:, 0:1] > level_of)).astype(f32)
    pack_u = lon_pack(2)
    edge_speed = 0.5 * (pack_u + left(pack_u, 1)) * edge_wet
    for q in range(4):
        pack = lon_pack(q)
        d = left(pack, 1) - pack
        extra_lon[q] = face_flux(edge_speed, pack, left(pack, 1), right(d, 2), right(d, 1), d, left(d, 1),
                                 left(d, 2))

    level_row = lax.broadcasted_iota(jnp.int32, (nlev, cols), 0).astype(f32)
    row_wet = ((sa[3, 0, SUB - 1:SUB, :] > level_row) & (sa[3, 0, SUB:SUB + 1, :] > level_row)).astype(f32)
    row_speed = 0.5 * (ext[3, :, SUB - 1, :] + ext[3, :, SUB, :]) * row_wet
    for q in range(4):
        cell = [ext[q, :, SUB - 3 + i, :] for i in range(6)]
        d = [cell[i + 1] - cell[i] for i in range(5)]
        extra_lat[q] = face_flux(row_speed, cell[2], cell[3], *d)

    def beside(q, k):
        both = jnp.where(spot < 3, lon_in[0, q], lon_in[1, q])
        return pltpu.roll(both, cols - 3 - wide * k, axis=1)

    def following(c, h):
        return left(jnp.where(lane == 0, h, c), 1)

    def advect(q, k, s_lon, s_south, s_north, slot):
        c = ext[q, k, SUB:top, :]
        h = beside(q, k)
        c1 = following(c, h)
        d = c1 - c
        dh = following(h, c) - h
        flux = face_flux(
            s_lon, c, c1,
            right(jnp.where(lane >= cols - 2, dh, d), 2),
            right(jnp.where(lane >= cols - 1, dh, d), 1),
            d,
            left(jnp.where(lane < 1, dh, d), 1),
            left(jnp.where(lane < 2, dh, d), 2))
        edge = pltpu.roll(extra_lon[q], cols - 2 - wide * k, axis=1)
        along = flux - jnp.where(lane == 0, edge, right(flux, 1))
        fbuf[slot, SUB - 1:SUB, :] = extra_lat[q, pl.ds(k, 1), :]
        fbuf[slot, SUB:2 * SUB, :] = face_rows(q, k, s_south, SUB, SUB)
        fbuf[slot, inner:top - SUB, :] = flat[q, k]
        fbuf[slot, top - SUB:top, :] = face_rows(q, k, s_north, top - SUB, SUB)
        return along + (fbuf[slot, SUB:top, :] - fbuf[slot, SUB - 1:top - 1, :])

    row = lax.broadcasted_iota(jnp.int32, (rows, cols), 0)
    latitude = ((y * rows + row).astype(f32) + 0.5) / float(ny * rows)
    coriolis = jnp.sin(math.pi * latitude - 0.5 * math.pi)

    def density(t, s, wet):
        return wet * (-0.2 * t + 0.8 * s - 0.05 * t * t + 0.03 * t * s)

    def momentum_level(k, slot, carry):
        above, above_h, sum_u, sum_v, star_u, star_v = carry
        level = k.astype(f32)
        wet_full = (sa[3, 0] > level).astype(f32)
        wet = (sa[3, 0, SUB:top, :] > level).astype(f32)
        wet_h = (sa[3, 1, SUB:top, :] > level).astype(f32)
        rho = density(ext[0, k], ext[1, k], wet_full)
        above = above + rho
        pressure = thickness * (above - 0.5 * rho)
        rho_h = density(beside(0, k), beside(1, k), wet_h)
        above_h = above_h + rho_h
        pressure_h = thickness * (above_h - 0.5 * rho_h)
        pbuf[slot] = pressure
        p = pbuf[slot, SUB:top, :]
        grad_lon = 0.5 * (following(p, pressure_h) - right(jnp.where(lane == cols - 1, pressure_h, p), 1))
        grad_lat = 0.5 * (pbuf[slot, SUB + 1:top + 1, :] - pbuf[slot, SUB - 1:top - 1, :])
        u = ext[2, k, SUB:top, :]
        v = ext[3, k, SUB:top, :]
        s_lon = 0.5 * (u + following(u, beside(2, k))) * wet * following(wet, wet_h)
        s_south = lat_speed(k, SUB, SUB)
        s_north = lat_speed(k, top - SUB, SUB)
        speed_lon[k] = s_lon
        speed_lat[0, k] = s_south
        speed_lat[1, k] = s_north
        accel_u = wet * (coriolis * v - advect(2, k, s_lon, s_south, s_north, 2 * slot) - grad_lon)
        accel_v = wet * (-advect(3, k, s_lon, s_south, s_north, 2 * slot + 1) - coriolis * u - grad_lat)
        u_star = wet * u + tracer_step * accel_u
        v_star = wet * v + tracer_step * accel_v
        out[2, k] = u_star
        out[3, k] = v_star
        return above, above_h, sum_u + accel_u, sum_v + accel_v, star_u + u_star, star_v + v_star

    def momentum(i, carry):
        for slot in range(2):
            carry = momentum_level(2 * i + slot, slot, carry)
        return carry

    zero = jnp.zeros((rows, cols), f32)
    _, _, sum_u, sum_v, star_u, star_v = lax.fori_loop(
        0, half, momentum, (jnp.zeros((full, cols), f32), zero, zero, zero, zero, zero))
    per_depth = thickness / jnp.maximum(thickness * sa[3, 0, SUB:top, :], thickness)
    sf[0, 0, SUB:top, :] = sum_u * per_depth
    sf[1, 0, SUB:top, :] = sum_v * per_depth
    mean_star_u = star_u * per_depth
    mean_star_v = star_v * per_depth
    force_lon_pair.start()

    def tracers(i, carry):
        for slot in range(2):
            k = 2 * i + slot
            wet = (sa[3, 0, SUB:top, :] > k.astype(f32)).astype(f32)
            for q in range(2):
                change = advect(q, k, speed_lon[k], speed_lat[0, k], speed_lat[1, k], 2 * slot + q)
                out[q, k] = wet * (ext[q, k, SUB:top, :] - tracer_step * change)
        return carry

    def store(q, k0, k1, sem):
        part = pltpu.make_async_copy(out.at[q:q + 2, k0:k1], out_hbm.at[q:q + 2, k0:k1], store_sem.at[sem])
        part.start()
        return part

    mid = half // 2
    lax.fori_loop(0, mid, tracers, 0)
    force_lon_pair.wait_recv()
    close_lon(sf, sf_lon, 2)
    stage_north(sf, sf_north, (-1.0, -1.0))
    force_lat_pair.start()
    stores = [store(0, 0, 2 * mid, 0)]
    lax.fori_loop(mid, half, tracers, 0)
    stores.append(store(0, 2 * mid, nlev, 1))
    force_lat_pair.wait_recv()

    def slope_lon(c, h):
        up_c = left(jnp.where(lane_full == 0, h, c), 1)
        up_h = left(jnp.where(lane_full == 0, c, h), 1)
        down_c = right(jnp.where(lane_full == cols - 1, h, c), 1)
        down_h = right(jnp.where(lane_full == cols - 1, c, h), 1)
        return 0.5 * (up_c - down_c), 0.5 * (up_h - down_h)

    def slope_lat(c, h):
        return tuple(0.5 * (pltpu.roll(a, full - 1, axis=0) - pltpu.roll(a, 1, axis=0)) for a in (c, h))

    both = (0, 1)
    height = [sa[0, i] for i in both]
    mean_u = [sa[1, i] for i in both]
    mean_v = [sa[2, i] for i in both]
    depth = [thickness * sa[3, i] for i in both]
    sea = [(sa[3, i] > 0.0).astype(f32) for i in both]
    for _ in range(NSUB):
        dx = slope_lon(*[depth[i] * mean_u[i] for i in both])
        dy = slope_lat(*[depth[i] * mean_v[i] for i in both])
        height = [sea[i] * (height[i] - surface_step * (dx[i] + dy[i])) for i in both]
        dx = slope_lon(*height)
        dy = slope_lat(*height)
        mean_u = [sea[i] * (mean_u[i] + surface_step * (sf[0, i] - dx[i])) for i in both]
        mean_v = [sea[i] * (mean_v[i] + surface_step * (sf[1, i] - dy[i])) for i in both]
    surf_out[0] = height[0][SUB:top]
    surf_out[1] = mean_u[0][SUB:top]
    surf_out[2] = mean_v[0][SUB:top]
    gain_u = mean_u[0][SUB:top] - mean_star_u
    gain_v = mean_v[0][SUB:top] - mean_star_v

    def finish(k0, k1):
        for k in range(k0, k1):
            wet = (sa[3, 0, SUB:top, :] > k).astype(f32)
            out[2, k] = wet * (out[2, k] + gain_u)
            out[3, k] = wet * (out[3, k] + gain_v)

    finish(0, half)
    stores.append(store(2, 0, half, 2))
    finish(half, nlev)
    stores.append(store(2, half, nlev, 3))
    for part in stores:
        part.wait()

    for pair in (surf_lon, level_lon, level_lat, surf_lat, force_lon_pair, force_lat_pair):
        pair.wait_send()


def on_device(nx, ny, ocean_state, surface_state, column_levels):
    _, nlev, rows, cols = ocean_state.shape
    if cols % 128 or nlev * 8 > cols or nlev % 4 or rows % SUB or rows < 3 * SUB or DEEP > SUB or nx % 2:
        raise ValueError("tile shape")
    full = rows + 2 * SUB
    vmem = pltpu.VMEM
    return pl.pallas_call(
        functools.partial(kernel, nx, ny),
        out_shape=(jax.ShapeDtypeStruct(ocean_state.shape, f32), jax.ShapeDtypeStruct(surface_state.shape, f32)),
        in_specs=[pl.BlockSpec(memory_space=pltpu.HBM)] * 3,
        out_specs=(pl.BlockSpec(memory_space=pl.ANY), pl.BlockSpec(memory_space=vmem)),
        scratch_shapes=[
            vmem((4, nlev, full, cols), f32),
            vmem((4, rows, cols), f32),
            vmem((2, 4, rows, cols), f32),
            vmem((2, 2 * nlev, SUB, cols), f32),
            vmem((2, 2 * nlev, SUB, cols), f32),
            vmem((4, 2, full, cols), f32),
            vmem((2, 2, full, cols), f32),
            vmem((2, 4, rows, cols), f32),
            vmem((2, 2, rows, cols), f32),
            vmem((4, 2, SUB, cols), f32),
            vmem((2, 2, SUB, cols), f32),
            vmem((4, rows, cols), f32),
            vmem((4, nlev, cols), f32),
            vmem((nlev, rows, cols), f32),
            vmem((2, nlev, SUB, cols), f32),
            vmem((2, full, cols), f32),
            vmem((4, full, cols), f32),
            vmem((4, nlev, rows - 2 * SUB, cols), f32),
            vmem((4, nlev, rows, cols), f32),
            vmem((rows, cols), jnp.int32),
            pltpu.SemaphoreType.DMA((3,)),
            pltpu.SemaphoreType.DMA((4,)),
            pltpu.SemaphoreType.DMA((12,)),
            pltpu.SemaphoreType.DMA((12,)),
        ],
        compiler_params=pltpu.CompilerParams(collective_id=0, has_side_effects=True),
    )(ocean_state, surface_state, column_levels)


def solution(mesh):
    return jax.shard_map(
        functools.partial(on_device, mesh.shape["lon"], mesh.shape["lat"]),
        mesh=mesh,
        in_specs=(P(None, None, "lat", "lon"), P(None, "lat", "lon"), P("lat", "lon")),
        out_specs=(P(None, None, "lat", "lon"), P(None, "lat", "lon")),
        check_vma=False,
    )
```

```python
import functools
import math

import jax
import jax.numpy as jnp
from jax import lax
from jax.experimental import pallas as pl
from jax.experimental.pallas import tpu as pltpu
from jax.sharding import PartitionSpec as P

NSUB = 4
DEEP = 2 * NSUB
SUB = 8
epsilon = 1e-06
tracer_step = 0.1
surface_step = 1.2
f32 = jnp.float32


def face_flux(s, q0, q1, dm2, dm1, d0, dp1, dp2):
    pos = s >= 0.0
    sixth = jnp.abs(s) * (1.0 / 6.0)
    c = jnp.where(pos, q0, q1)
    d1 = jnp.where(pos, dm2, dp2)
    d2 = jnp.where(pos, dm1, dp1)
    d3 = d0
    d4 = jnp.where(pos, dp1, dm1)
    k = 13.0 / 3.0
    b1 = d2 - d1
    b2 = d3 - d2
    b3 = d4 - d3
    t1 = 3.0 * d2 - d1
    t2 = d2 + d3
    t3 = d4 - 3.0 * d3
    s1 = (k * b1) * b1 + t1 * t1 + 4.0 * epsilon
    s2 = (k * b2) * b2 + t2 * t2 + 4.0 * epsilon
    s3 = (k * b3) * b3 + t3 * t3 + 4.0 * epsilon
    p23 = s2 * s3
    p13 = s1 * s3
    p12 = s1 * s2
    w1 = p23 * p23
    w2 = 6.0 * (p13 * p13)
    w3 = 3.0 * (p12 * p12)
    top = w1 * (2.0 * t1 - d2) + w2 * (t2 + d3) + w3 * (d3 - t3)
    return s * c + sixth * (top * pl.reciprocal(w1 + w2 + w3, approx=True))


def left(x, n):
    return pltpu.roll(x, x.shape[-1] - n, axis=x.ndim - 1)


def right(x, n):
    return pltpu.roll(x, n, axis=x.ndim - 1)


def kernel(nx, ny, ocean, surface, levels_in, out_hbm, gain, surf_out, ext, lon_own, lon_in, lat_out, lat_in, sa, sf,
           sa_lon, sf_lon, sa_north, sf_north, extra_lon, extra_lat, speed_lon, speed_lat, pbuf, fbuf,
           flat, out, counts, local_sem, store_sem, send_sem, recv_sem):
    nlev, rows, cols = ocean.shape[1], ocean.shape[2], ocean.shape[3]
    top = SUB + rows
    full = top + SUB
    thickness = 1.0 / nlev
    wide = 8
    x = lax.axis_index("lon")
    y = lax.axis_index("lat")
    at_north = y == ny - 1
    east = {"lon": lax.rem(x + 1, nx), "lat": y}
    west = {"lon": lax.rem(x + nx - 1, nx), "lat": y}
    north = {"lon": jnp.where(at_north, nx - 1 - x, x), "lat": jnp.where(at_north, y, y + 1)}
    south = {"lon": x, "lat": jnp.maximum(y - 1, 0)}
    fold = jnp.where(at_north, 1, 0)
    far_row = pl.multiple_of(fold * top, SUB)

    load = pltpu.make_async_copy(ocean, ext.at[:, :, SUB:top, :], local_sem.at[0])
    load_surface = pltpu.make_async_copy(surface, sa.at[0:3, 0, SUB:top, :], local_sem.at[1])
    load_counts = pltpu.make_async_copy(levels_in, counts, local_sem.at[2])
    load.start()
    load_surface.start()
    load_counts.start()

    @pl.when(y == 0)
    def _():
        sa[:, :, 0:SUB, :] = jnp.zeros((4, 2, SUB, cols), f32)
        sf[:, :, 0:SUB, :] = jnp.zeros((2, 2, SUB, cols), f32)
        lat_in[0] = jnp.zeros(lat_in.shape[1:], f32)

    barrier = pltpu.get_barrier_semaphore()
    for target in (east, west, north):
        pl.semaphore_signal(barrier, inc=1, device_id=target, device_id_type=pl.DeviceIdType.MESH)

    @pl.when(y > 0)
    def _():
        pl.semaphore_signal(barrier, inc=1, device_id=south, device_id_type=pl.DeviceIdType.MESH)

    def remote(src, dst, send, recv, target):
        return pltpu.make_async_remote_copy(
            src_ref=src, dst_ref=dst, send_sem=send_sem.at[send], recv_sem=recv_sem.at[recv],
            device_id=target, device_id_type=pl.DeviceIdType.MESH)

    class LonPair:
        def __init__(self, src, dst, base):
            self.go_east = remote(src, dst.at[0], base, base, east)
            self.go_west = remote(src, dst.at[1], base + 1, base + 1, west)

        def start(self):
            self.go_east.start()
            self.go_west.start()

        def wait_recv(self):
            self.go_east.wait_recv()
            self.go_west.wait_recv()

        def wait_send(self):
            self.go_east.wait_send()
            self.go_west.wait_send()

    class LatPair:
        def __init__(self, north_src, north_dst, south_src, dst_south, dst_north, base):
            self.go_north = remote(north_src, north_dst, base, base + fold, north)
            self.go_south = remote(south_src, dst_north, base + 1, base + 1, south)
            self.from_south = remote(north_src, dst_south, base, base, south)

        def start(self):
            self.go_north.start()

            @pl.when(y > 0)
            def _():
                self.go_south.start()

        def wait_recv(self):
            self.go_south.wait_recv()

            @pl.when(y > 0)
            def _():
                self.from_south.wait_recv()

        def wait_send(self):
            self.go_north.wait_send()

            @pl.when(y > 0)
            def _():
                self.go_south.wait_send()

    surf_lon = LonPair(sa.at[:, 0, SUB:top, :], sa_lon, 0)
    level_lon = LonPair(lon_own, lon_in, 2)
    force_lon_pair = LonPair(sf.at[:, 0, SUB:top, :], sf_lon, 4)
    level_lat = LatPair(lat_out.at[0], lat_in.at[fold], lat_out.at[1], lat_in.at[0], lat_in.at[1], 6)
    surf_lat = LatPair(sa_north, sa.at[:, :, pl.ds(far_row, SUB), :], sa.at[:, :, SUB:2 * SUB, :],
                       sa.at[:, :, 0:SUB, :], sa.at[:, :, top:full, :], 8)
    force_lat_pair = LatPair(sf_north, sf.at[:, :, pl.ds(far_row, SUB), :], sf.at[:, :, SUB:2 * SUB, :],
                             sf.at[:, :, 0:SUB, :], sf.at[:, :, top:full, :], 10)

    lane = lax.broadcasted_iota(jnp.int32, (rows, cols), 1)
    lane_full = lax.broadcasted_iota(jnp.int32, (full, cols), 1)
    spot = lane % wide
    owner = lane // wide
    sub8 = lax.broadcasted_iota(jnp.int32, (SUB, cols), 0)

    def mirrored(block):
        count = block.shape[0]
        a = lax.broadcasted_iota(jnp.int32, (cols, cols), 0)
        b = lax.broadcasted_iota(jnp.int32, (cols, cols), 1)
        flip_cols = (a + b == cols - 1).astype(f32)
        a = lax.broadcasted_iota(jnp.int32, (count, count), 0)
        b = lax.broadcasted_iota(jnp.int32, (count, count), 1)
        flip_rows = ((a // SUB == b // SUB) & (a % SUB + b % SUB == SUB - 1)).astype(f32)
        block = lax.dot(block, flip_cols, precision=lax.Precision.HIGHEST, preferred_element_type=f32)
        return lax.dot(flip_rows, block, precision=lax.Precision.HIGHEST, preferred_element_type=f32)

    load.wait()
    half = nlev // 2
    for q in range(4):
        for h in range(half):
            n0 = ext[q, 2 * h, top - SUB:top, :]
            n1 = ext[q, 2 * h + 1, top - SUB:top, :]
            lat_out[0, q * half + h] = jnp.where(sub8 >= 4, n0, pltpu.roll(n1, 4, axis=0))
            s0 = ext[q, 2 * h, SUB:2 * SUB, :]
            s1 = ext[q, 2 * h + 1, SUB:2 * SUB, :]
            lat_out[1, q * half + h] = jnp.where(sub8 < 4, s0, pltpu.roll(s1, 4, axis=0))

    @pl.when(at_north)
    def _():
        for q in range(4):
            sign = 1.0 if q < 2 else -1.0
            block = lat_out[0, q * half:(q + 1) * half].reshape(half * SUB, cols)
            lat_out[0, q * half:(q + 1) * half] = (sign * mirrored(block)).reshape(half, SUB, cols)

    load_surface.wait()
    load_counts.wait()
    sa[3, 0, SUB:top, :] = counts[...].astype(f32)
    pl.semaphore_wait(barrier, 3 + jnp.where(y > 0, 1, 0))
    surf_lon.start()
    level_lat.start()

    for q in range(4):
        pack = jnp.zeros((rows, cols), f32)
        for k in range(nlev):
            pack = jnp.where(owner == k, right(ext[q, k, SUB:top, :], wide * k + 3), pack)
        lon_own[q] = pack
    level_lon.start()

    def close_lon(fields, arrived, count):
        for f in range(count):
            fields[f, 1, SUB:top, :] = jnp.where(lane < cols // 2, arrived[1, f], arrived[0, f])

    def stage_north(fields, staged, signs):
        count = len(signs)
        for f in range(count):
            for part in range(2):
                staged[f, part] = fields[f, part, top - SUB:top, :]

        @pl.when(at_north)
        def _():
            for f in range(count):
                block = staged[f].reshape(2 * SUB, cols)
                staged[f] = (signs[f] * mirrored(block)).reshape(2, SUB, cols)

    surf_lon.wait_recv()
    close_lon(sa, sa_lon, 4)
    stage_north(sa, sa_north, (1.0, -1.0, -1.0, 1.0))
    surf_lat.start()

    def face_rows(q, k, s, first, count):
        start = first - 2 + jnp.minimum(k, 0)
        cell = [ext[q, k, pl.ds(start + i, count), :] for i in range(6)]
        return face_flux(s, cell[2], cell[3], *[cell[i + 1] - cell[i] for i in range(5)])

    def lat_speed(k, first, count):
        level = k.astype(f32)
        wet = (sa[3, 0, first:first + count, :] > level).astype(f32)
        wet_up = (sa[3, 0, first + 1:first + 1 + count, :] > level).astype(f32)
        return 0.5 * (ext[3, k, first:first + count, :] + ext[3, k, first + 1:first + 1 + count, :]) * wet * wet_up

    inner, inner_count = 2 * SUB, rows - 2 * SUB

    def inner_faces(i, carry):
        for k in (2 * i, 2 * i + 1):
            s = lat_speed(k, inner, inner_count)
            for q in range(4):
                flat[q, k] = face_rows(q, k, s, inner, inner_count)
        return carry

    lax.fori_loop(0, half, inner_faces, 0)

    level_lon.wait_recv()
    level_lat.wait_recv()
    surf_lat.wait_recv()

    for q in range(4):
        for h in range(half):
            for side, place in ((0, 0), (1, top)):
                block = lat_in[side, q * half + h]
                ext[q, 2 * h, place:place + SUB, :] = block
                ext[q, 2 * h + 1, place:place + SUB, :] = pltpu.roll(block, 4, axis=0)

    def lon_pack(q):
        return jnp.where(spot < 3, lon_in[0, q], lon_own[q])

    count_here = sa[3, 0, SUB:top, :]
    count_beside = sa[3, 1, SUB:top, :]
    level_of = owner.astype(f32)
    edge_wet = ((count_beside[:, cols - 1:cols] > level_of) & (count_here[:, 0:1] > level_of)).astype(f32)
    pack_u = lon_pack(2)
    edge_speed = 0.5 * (pack_u + left(pack_u, 1)) * edge_wet
    for q in range(4):
        pack = lon_pack(q)
        d = left(pack, 1) - pack
        extra_lon[q] = face_flux(edge_speed, pack, left(pack, 1), right(d, 2), right(d, 1), d, left(d, 1),
                                 left(d, 2))

    level_row = lax.broadcasted_iota(jnp.int32, (nlev, cols), 0).astype(f32)
    row_wet = ((sa[3, 0, SUB - 1:SUB, :] > level_row) & (sa[3, 0, SUB:SUB + 1, :] > level_row)).astype(f32)
    row_speed = 0.5 * (ext[3, :, SUB - 1, :] + ext[3, :, SUB, :]) * row_wet
    for q in range(4):
        cell = [ext[q, :, SUB - 3 + i, :] for i in range(6)]
        d = [cell[i + 1] - cell[i] for i in range(5)]
        extra_lat[q] = face_flux(row_speed, cell[2], cell[3], *d)

    def beside(q, k):
        both = jnp.where(spot < 3, lon_in[0, q], lon_in[1, q])
        return pltpu.roll(both, cols - 3 - wide * k, axis=1)

    def following(c, h):
        return left(jnp.where(lane == 0, h, c), 1)

    def advect(q, k, s_lon, s_south, s_north, slot):
        c = ext[q, k, SUB:top, :]
        h = beside(q, k)
        c1 = following(c, h)
        d = c1 - c
        dh = following(h, c) - h
        flux = face_flux(
            s_lon, c, c1,
            right(jnp.where(lane >= cols - 2, dh, d), 2),
            right(jnp.where(lane >= cols - 1, dh, d), 1),
            d,
            left(jnp.where(lane < 1, dh, d), 1),
            left(jnp.where(lane < 2, dh, d), 2))
        edge = pltpu.roll(extra_lon[q], cols - 2 - wide * k, axis=1)
        along = flux - jnp.where(lane == 0, edge, right(flux, 1))
        fbuf[slot, SUB - 1:SUB, :] = extra_lat[q, pl.ds(k, 1), :]
        fbuf[slot, SUB:2 * SUB, :] = face_rows(q, k, s_south, SUB, SUB)
        fbuf[slot, inner:top - SUB, :] = flat[q, k]
        fbuf[slot, top - SUB:top, :] = face_rows(q, k, s_north, top - SUB, SUB)
        return along + (fbuf[slot, SUB:top, :] - fbuf[slot, SUB - 1:top - 1, :])

    row = lax.broadcasted_iota(jnp.int32, (rows, cols), 0)
    latitude = ((y * rows + row).astype(f32) + 0.5) / float(ny * rows)
    coriolis = jnp.sin(math.pi * latitude - 0.5 * math.pi)

    def density(t, s, wet):
        return wet * (-0.2 * t + 0.8 * s - 0.05 * t * t + 0.03 * t * s)

    def momentum_level(k, slot, carry):
        above, above_h, sum_u, sum_v, star_u, star_v = carry
        level = k.astype(f32)
        wet_full = (sa[3, 0] > level).astype(f32)
        wet = (sa[3, 0, SUB:top, :] > level).astype(f32)
        wet_h = (sa[3, 1, SUB:top, :] > level).astype(f32)
        rho = density(ext[0, k], ext[1, k], wet_full)
        above = above + rho
        pressure = thickness * (above - 0.5 * rho)
        rho_h = density(beside(0, k), beside(1, k), wet_h)
        above_h = above_h + rho_h
        pressure_h = thickness * (above_h - 0.5 * rho_h)
        pbuf[slot] = pressure
        p = pbuf[slot, SUB:top, :]
        grad_lon = 0.5 * (following(p, pressure_h) - right(jnp.where(lane == cols - 1, pressure_h, p), 1))
        grad_lat = 0.5 * (pbuf[slot, SUB + 1:top + 1, :] - pbuf[slot, SUB - 1:top - 1, :])
        u = ext[2, k, SUB:top, :]
        v = ext[3, k, SUB:top, :]
        s_lon = 0.5 * (u + following(u, beside(2, k))) * wet * following(wet, wet_h)
        s_south = lat_speed(k, SUB, SUB)
        s_north = lat_speed(k, top - SUB, SUB)
        speed_lon[k] = s_lon
        speed_lat[0, k] = s_south
        speed_lat[1, k] = s_north
        accel_u = wet * (coriolis * v - advect(2, k, s_lon, s_south, s_north, 2 * slot) - grad_lon)
        accel_v = wet * (-advect(3, k, s_lon, s_south, s_north, 2 * slot + 1) - coriolis * u - grad_lat)
        u_star = wet * u + tracer_step * accel_u
        v_star = wet * v + tracer_step * accel_v
        out[2, k] = u_star
        out[3, k] = v_star
        return above, above_h, sum_u + accel_u, sum_v + accel_v, star_u + u_star, star_v + v_star

    def momentum(i, carry):
        for slot in range(2):
            carry = momentum_level(2 * i + slot, slot, carry)
        return carry

    zero = jnp.zeros((rows, cols), f32)
    _, _, sum_u, sum_v, star_u, star_v = lax.fori_loop(
        0, half, momentum, (jnp.zeros((full, cols), f32), zero, zero, zero, zero, zero))
    per_depth = thickness / jnp.maximum(thickness * sa[3, 0, SUB:top, :], thickness)
    sf[0, 0, SUB:top, :] = sum_u * per_depth
    sf[1, 0, SUB:top, :] = sum_v * per_depth
    mean_star_u = star_u * per_depth
    mean_star_v = star_v * per_depth
    force_lon_pair.start()

    def store(q, k0, k1, sem):
        part = pltpu.make_async_copy(out.at[q:q + 2, k0:k1], out_hbm.at[q:q + 2, k0:k1], store_sem.at[sem])
        part.start()
        return part

    stores = [store(2, 0, nlev, 0)]

    def tracers(i, carry):
        for slot in range(2):
            k = 2 * i + slot
            wet = (sa[3, 0, SUB:top, :] > k.astype(f32)).astype(f32)
            for q in range(2):
                change = advect(q, k, speed_lon[k], speed_lat[0, k], speed_lat[1, k], 2 * slot + q)
                out[q, k] = wet * (ext[q, k, SUB:top, :] - tracer_step * change)
        return carry

    mid = half // 2
    lax.fori_loop(0, mid, tracers, 0)
    force_lon_pair.wait_recv()
    close_lon(sf, sf_lon, 2)
    stage_north(sf, sf_north, (-1.0, -1.0))
    force_lat_pair.start()
    stores.append(store(0, 0, 2 * mid, 1))
    lax.fori_loop(mid, half, tracers, 0)
    stores.append(store(0, 2 * mid, nlev, 2))
    force_lat_pair.wait_recv()

    def slope_lon(c, h):
        up_c = left(jnp.where(lane_full == 0, h, c), 1)
        up_h = left(jnp.where(lane_full == 0, c, h), 1)
        down_c = right(jnp.where(lane_full == cols - 1, h, c), 1)
        down_h = right(jnp.where(lane_full == cols - 1, c, h), 1)
        return 0.5 * (up_c - down_c), 0.5 * (up_h - down_h)

    def slope_lat(c, h):
        return tuple(0.5 * (pltpu.roll(a, full - 1, axis=0) - pltpu.roll(a, 1, axis=0)) for a in (c, h))

    both = (0, 1)
    height = [sa[0, i] for i in both]
    mean_u = [sa[1, i] for i in both]
    mean_v = [sa[2, i] for i in both]
    depth = [thickness * sa[3, i] for i in both]
    sea = [(sa[3, i] > 0.0).astype(f32) for i in both]
    for _ in range(NSUB):
        dx = slope_lon(*[depth[i] * mean_u[i] for i in both])
        dy = slope_lat(*[depth[i] * mean_v[i] for i in both])
        height = [sea[i] * (height[i] - surface_step * (dx[i] + dy[i])) for i in both]
        dx = slope_lon(*height)
        dy = slope_lat(*height)
        mean_u = [sea[i] * (mean_u[i] + surface_step * (sf[0, i] - dx[i])) for i in both]
        mean_v = [sea[i] * (mean_v[i] + surface_step * (sf[1, i] - dy[i])) for i in both]
    surf_out[0] = height[0][SUB:top]
    surf_out[1] = mean_u[0][SUB:top]
    surf_out[2] = mean_v[0][SUB:top]
    gain[0] = zero
    gain[1] = zero
    gain[2] = mean_u[0][SUB:top] - mean_star_u
    gain[3] = mean_v[0][SUB:top] - mean_star_v
    for part in stores:
        part.wait()

    for pair in (surf_lon, level_lon, level_lat, surf_lat, force_lon_pair, force_lat_pair):
        pair.wait_send()


def on_device(nx, ny, ocean_state, surface_state, column_levels):
    _, nlev, rows, cols = ocean_state.shape
    if cols % 128 or nlev * 8 > cols or nlev % 4 or rows % SUB or rows < 3 * SUB or DEEP > SUB or nx % 2:
        raise ValueError("tile shape")
    full = rows + 2 * SUB
    vmem = pltpu.VMEM
    stars, gain, surface_next = pl.pallas_call(
        functools.partial(kernel, nx, ny),
        out_shape=(jax.ShapeDtypeStruct(ocean_state.shape, f32), jax.ShapeDtypeStruct((4, rows, cols), f32),
                   jax.ShapeDtypeStruct(surface_state.shape, f32)),
        in_specs=[pl.BlockSpec(memory_space=pltpu.HBM)] * 3,
        out_specs=(pl.BlockSpec(memory_space=pl.ANY), pl.BlockSpec(memory_space=vmem), pl.BlockSpec(memory_space=vmem)),
        scratch_shapes=[
            vmem((4, nlev, full, cols), f32),
            vmem((4, rows, cols), f32),
            vmem((2, 4, rows, cols), f32),
            vmem((2, 2 * nlev, SUB, cols), f32),
            vmem((2, 2 * nlev, SUB, cols), f32),
            vmem((4, 2, full, cols), f32),
            vmem((2, 2, full, cols), f32),
            vmem((2, 4, rows, cols), f32),
            vmem((2, 2, rows, cols), f32),
            vmem((4, 2, SUB, cols), f32),
            vmem((2, 2, SUB, cols), f32),
            vmem((4, rows, cols), f32),
            vmem((4, nlev, cols), f32),
            vmem((nlev, rows, cols), f32),
            vmem((2, nlev, SUB, cols), f32),
            vmem((2, full, cols), f32),
            vmem((4, full, cols), f32),
            vmem((4, nlev, rows - 2 * SUB, cols), f32),
            vmem((4, nlev, rows, cols), f32),
            vmem((rows, cols), jnp.int32),
            pltpu.SemaphoreType.DMA((3,)),
            pltpu.SemaphoreType.DMA((3,)),
            pltpu.SemaphoreType.DMA((12,)),
            pltpu.SemaphoreType.DMA((12,)),
        ],
        compiler_params=pltpu.CompilerParams(collective_id=0, has_side_effects=True),
    )(ocean_state, surface_state, column_levels)
    level = lax.broadcasted_iota(jnp.int32, stars.shape, 1)
    return jnp.where(level < column_levels, stars + gain[:, None], 0.0), surface_next


def solution(mesh):
    return jax.shard_map(
        functools.partial(on_device, mesh.shape["lon"], mesh.shape["lat"]),
        mesh=mesh,
        in_specs=(P(None, None, "lat", "lon"), P(None, "lat", "lon"), P("lat", "lon")),
        out_specs=(P(None, None, "lat", "lon"), P(None, "lat", "lon")),
        check_vma=False,
    )
```

```python
import functools
import math

import jax
import jax.numpy as jnp
from jax import lax
from jax.experimental import pallas as pl
from jax.experimental.pallas import tpu as pltpu
from jax.sharding import PartitionSpec as P

NSUB = 4
DEEP = 2 * NSUB
SUB = 8
epsilon = 1e-06
tracer_step = 0.1
surface_step = 1.2
f32 = jnp.float32


def face_flux(s, q0, q1, dm2, dm1, d0, dp1, dp2):
    pos = s >= 0.0
    third = jnp.abs(s) * (1.0 / 3.0)
    c = jnp.where(pos, q0, q1)
    d1 = jnp.where(pos, dm2, dp2)
    d2 = jnp.where(pos, dm1, dp1)
    d3 = d0
    d4 = jnp.where(pos, dp1, dm1)
    rest2 = ((39.0 / 64.0) * d2) * d2 + 0.75 * epsilon
    rest3 = ((39.0 / 64.0) * d3) * d3 + 0.75 * epsilon
    g1 = d1 - (11.0 / 8.0) * d2
    g2 = d2 - (5.0 / 8.0) * d3
    g3 = d4 - (11.0 / 8.0) * d3
    s1 = g1 * g1 + rest2
    s2 = g2 * g2 + rest3
    s3 = g3 * g3 + rest3
    p23 = s2 * s3
    p13 = s1 * s3
    p12 = s1 * s2
    w1 = (p23 * (1.0 / 3.0)) * p23
    w2 = p13 * p13
    w3 = p12 * p12
    twice = d3 + d3
    top = w1 * (2.5 * d2 - d1) + w2 * (d2 + twice) + w3 * (twice - 0.5 * d4)
    total = (w1 + w2) + (w2 + w3)
    return s * c + third * (top * pl.reciprocal(total, approx=True))


def left(x, n):
    return pltpu.roll(x, x.shape[-1] - n, axis=x.ndim - 1)


def right(x, n):
    return pltpu.roll(x, n, axis=x.ndim - 1)


def kernel(nx, ny, ocean, surface, levels_in, out_hbm, gain, surf_out, ext, lon_own, lon_in, lat_out, lat_in, sa, sf,
           sa_lon, sf_lon, sa_north, sf_north, extra_lon, extra_lat, speed_lon, speed_lat, pbuf, fbuf,
           flat, out, counts, crow, lon_both, local_sem, store_sem, send_sem, recv_sem):
    nlev, rows, cols = ocean.shape[1], ocean.shape[2], ocean.shape[3]
    top = SUB + rows
    full = top + SUB
    thickness = 1.0 / nlev
    wide = 8
    x = lax.axis_index("lon")
    y = lax.axis_index("lat")
    at_north = y == ny - 1
    east = {"lon": lax.rem(x + 1, nx), "lat": y}
    west = {"lon": lax.rem(x + nx - 1, nx), "lat": y}
    north = {"lon": jnp.where(at_north, nx - 1 - x, x), "lat": jnp.where(at_north, y, y + 1)}
    south = {"lon": x, "lat": jnp.maximum(y - 1, 0)}
    fold = jnp.where(at_north, 1, 0)
    far_row = pl.multiple_of(fold * top, SUB)

    load = pltpu.make_async_copy(ocean, ext.at[:, :, SUB:top, :], local_sem.at[0])
    load_surface = pltpu.make_async_copy(surface, sa.at[0:3, 0, SUB:top, :], local_sem.at[1])
    load_counts = pltpu.make_async_copy(levels_in, counts, local_sem.at[2])
    load.start()
    load_surface.start()
    load_counts.start()

    @pl.when(y == 0)
    def _():
        sa[:, :, 0:SUB, :] = jnp.zeros((4, 2, SUB, cols), f32)
        sf[:, :, 0:SUB, :] = jnp.zeros((2, 2, SUB, cols), f32)
        lat_in[0] = jnp.zeros(lat_in.shape[1:], f32)

    barrier = pltpu.get_barrier_semaphore()
    for target in (east, west, north):
        pl.semaphore_signal(barrier, inc=1, device_id=target, device_id_type=pl.DeviceIdType.MESH)

    @pl.when(y > 0)
    def _():
        pl.semaphore_signal(barrier, inc=1, device_id=south, device_id_type=pl.DeviceIdType.MESH)

    def remote(src, dst, send, recv, target):
        return pltpu.make_async_remote_copy(
            src_ref=src, dst_ref=dst, send_sem=send_sem.at[send], recv_sem=recv_sem.at[recv],
            device_id=target, device_id_type=pl.DeviceIdType.MESH)

    class LonPair:
        def __init__(self, src, dst, base):
            self.go_east = remote(src, dst.at[0], base, base, east)
            self.go_west = remote(src, dst.at[1], base + 1, base + 1, west)

        def start(self):
            self.go_east.start()
            self.go_west.start()

        def wait_recv(self):
            self.go_east.wait_recv()
            self.go_west.wait_recv()

        def wait_send(self):
            self.go_east.wait_send()
            self.go_west.wait_send()

    class LatPair:
        def __init__(self, north_src, north_dst, south_src, dst_south, dst_north, base):
            self.go_north = remote(north_src, north_dst, base, base + fold, north)
            self.go_south = remote(south_src, dst_north, base + 1, base + 1, south)
            self.from_south = remote(north_src, dst_south, base, base, south)

        def start(self):
            self.go_north.start()

            @pl.when(y > 0)
            def _():
                self.go_south.start()

        def wait_recv(self):
            self.go_south.wait_recv()

            @pl.when(y > 0)
            def _():
                self.from_south.wait_recv()

        def wait_send(self):
            self.go_north.wait_send()

            @pl.when(y > 0)
            def _():
                self.go_south.wait_send()

    surf_lon = LonPair(sa.at[:, 0, SUB:top, :], sa_lon, 0)
    level_lon = LonPair(lon_own, lon_in, 2)
    force_lon_pair = LonPair(sf.at[:, 0, SUB:top, :], sf_lon, 4)
    level_lat = LatPair(lat_out.at[0], lat_in.at[fold], lat_out.at[1], lat_in.at[0], lat_in.at[1], 6)
    surf_lat = LatPair(sa_north, sa.at[:, :, pl.ds(far_row, SUB), :], sa.at[:, :, SUB:2 * SUB, :],
                       sa.at[:, :, 0:SUB, :], sa.at[:, :, top:full, :], 8)
    force_lat_pair = LatPair(sf_north, sf.at[:, :, pl.ds(far_row, SUB), :], sf.at[:, :, SUB:2 * SUB, :],
                             sf.at[:, :, 0:SUB, :], sf.at[:, :, top:full, :], 10)

    lane = lax.broadcasted_iota(jnp.int32, (rows, cols), 1)
    lane_full = lax.broadcasted_iota(jnp.int32, (full, cols), 1)
    spot = lane % wide
    owner = lane // wide
    sub8 = lax.broadcasted_iota(jnp.int32, (SUB, cols), 0)

    def mirrored(block):
        for axis, length in ((0, SUB), (1, cols)):
            at = lax.broadcasted_iota(jnp.int32, block.shape, axis)
            size = block.shape[axis]
            step = 1
            while step < length:
                up = pltpu.roll(block, step, axis=axis)
                down = pltpu.roll(block, size - step, axis=axis)
                block = jnp.where((at // step) % 2 == 1, up, down)
                step *= 2
        return block

    load.wait()
    half = nlev // 2
    for q in range(4):
        for h in range(half):
            n0 = ext[q, 2 * h, top - SUB:top, :]
            n1 = ext[q, 2 * h + 1, top - SUB:top, :]
            lat_out[0, q * half + h] = jnp.where(sub8 >= 4, n0, pltpu.roll(n1, 4, axis=0))
            s0 = ext[q, 2 * h, SUB:2 * SUB, :]
            s1 = ext[q, 2 * h + 1, SUB:2 * SUB, :]
            lat_out[1, q * half + h] = jnp.where(sub8 < 4, s0, pltpu.roll(s1, 4, axis=0))

    load_surface.wait()
    load_counts.wait()
    sa[3, 0, SUB:top, :] = counts[...].astype(f32)
    crow[SUB:top, :] = sa[3, 0, SUB:top, :]
    lat_out[0, 4 * half] = crow[top - SUB:top, :]
    lat_out[1, 4 * half] = crow[SUB:2 * SUB, :]

    @pl.when(at_north)
    def _():
        lat_out[0, 4 * half] = mirrored(lat_out[0, 4 * half])
        for q in range(4):
            sign = 1.0 if q < 2 else -1.0
            block = lat_out[0, q * half:(q + 1) * half].reshape(half * SUB, cols)
            lat_out[0, q * half:(q + 1) * half] = (sign * mirrored(block)).reshape(half, SUB, cols)

    pl.semaphore_wait(barrier, 3 + jnp.where(y > 0, 1, 0))
    surf_lon.start()
    level_lat.start()

    for q in range(4):
        pack = jnp.zeros((rows, cols), f32)
        for k in range(nlev):
            pack = jnp.where(owner == k, right(ext[q, k, SUB:top, :], wide * k + 3), pack)
        lon_own[q] = pack
    level_lon.start()

    def close_lon(fields, arrived, count):
        for f in range(count):
            fields[f, 1, SUB:top, :] = jnp.where(lane < cols // 2, arrived[1, f], arrived[0, f])

    def stage_north(fields, staged, signs):
        count = len(signs)
        for f in range(count):
            for part in range(2):
                staged[f, part] = fields[f, part, top - SUB:top, :]

        @pl.when(at_north)
        def _():
            for f in range(count):
                block = staged[f].reshape(2 * SUB, cols)
                staged[f] = (signs[f] * mirrored(block)).reshape(2, SUB, cols)

    def face_rows(q, k, s, first, count):
        start = first - 2 + jnp.minimum(k, 0)
        cell = [ext[q, k, pl.ds(start + i, count), :] for i in range(6)]
        return face_flux(s, cell[2], cell[3], *[cell[i + 1] - cell[i] for i in range(5)])

    def lat_speed(k, first, count):
        least = jnp.minimum(crow[first:first + count, :], crow[first + 1:first + 1 + count, :])
        speed = 0.5 * (ext[3, k, first:first + count, :] + ext[3, k, first + 1:first + 1 + count, :])
        return jnp.where(least > k.astype(f32), speed, 0.0)

    inner, inner_count = 2 * SUB, rows - 2 * SUB

    def inner_faces(i, carry):
        for k in (2 * i, 2 * i + 1):
            s = lat_speed(k, inner, inner_count)
            for q in range(4):
                flat[q, k] = face_rows(q, k, s, inner, inner_count)
        return carry

    lax.fori_loop(0, half, inner_faces, 0)

    surf_lon.wait_recv()
    close_lon(sa, sa_lon, 4)
    stage_north(sa, sa_north, (1.0, -1.0, -1.0, 1.0))
    surf_lat.start()

    level_lon.wait_recv()
    level_lat.wait_recv()
    crow[0:SUB, :] = lat_in[0, 4 * half]
    crow[top:full, :] = lat_in[1, 4 * half]

    for q in range(4):
        for h in range(half):
            for side, place in ((0, 0), (1, top)):
                block = lat_in[side, q * half + h]
                ext[q, 2 * h, place:place + SUB, :] = block
                ext[q, 2 * h + 1, place:place + SUB, :] = pltpu.roll(block, 4, axis=0)

    def lon_pack(q):
        return jnp.where(spot < 3, lon_in[0, q], lon_own[q])

    count_here = crow[SUB:top, :]
    count_beside = sa[3, 1, SUB:top, :]
    level_of = owner.astype(f32)
    for q in range(4):
        lon_both[q] = jnp.where(spot < 3, lon_in[0, q], lon_in[1, q])
    edge_wet = ((count_beside[:, cols - 1:cols] > level_of) & (count_here[:, 0:1] > level_of)).astype(f32)
    pack_u = lon_pack(2)
    edge_speed = 0.5 * (pack_u + left(pack_u, 1)) * edge_wet
    for q in range(4):
        pack = lon_pack(q)
        d = left(pack, 1) - pack
        extra_lon[q] = face_flux(edge_speed, pack, left(pack, 1), right(d, 2), right(d, 1), d, left(d, 1),
                                 left(d, 2))

    level_row = lax.broadcasted_iota(jnp.int32, (nlev, cols), 0).astype(f32)
    row_wet = ((crow[SUB - 1:SUB, :] > level_row) & (crow[SUB:SUB + 1, :] > level_row)).astype(f32)
    row_speed = 0.5 * (ext[3, :, SUB - 1, :] + ext[3, :, SUB, :]) * row_wet
    for q in range(4):
        cell = [ext[q, :, SUB - 3 + i, :] for i in range(6)]
        d = [cell[i + 1] - cell[i] for i in range(5)]
        extra_lat[q] = face_flux(row_speed, cell[2], cell[3], *d)

    def beside(q, k):
        return pltpu.roll(lon_both[q], cols - 3 - wide * k, axis=1)

    def following(c, h):
        return left(jnp.where(lane == 0, h, c), 1)

    def advect(q, k, s_lon, s_south, s_north, slot):
        c = ext[q, k, SUB:top, :]
        h = beside(q, k)
        c1 = following(c, h)
        d = c1 - c
        dh = following(h, c) - h
        flux = face_flux(
            s_lon, c, c1,
            right(jnp.where(lane >= cols - 2, dh, d), 2),
            right(jnp.where(lane >= cols - 1, dh, d), 1),
            d,
            left(jnp.where(lane < 1, dh, d), 1),
            left(jnp.where(lane < 2, dh, d), 2))
        edge = pltpu.roll(extra_lon[q], cols - 2 - wide * k, axis=1)
        along = flux - jnp.where(lane == 0, edge, right(flux, 1))
        fbuf[slot, SUB - 1:SUB, :] = extra_lat[q, pl.ds(k, 1), :]
        fbuf[slot, SUB:2 * SUB, :] = face_rows(q, k, s_south, SUB, SUB)
        fbuf[slot, inner:top - SUB, :] = flat[q, k]
        fbuf[slot, top - SUB:top, :] = face_rows(q, k, s_north, top - SUB, SUB)
        return along + (fbuf[slot, SUB:top, :] - fbuf[slot, SUB - 1:top - 1, :])

    row = lax.broadcasted_iota(jnp.int32, (rows, cols), 0)
    latitude = ((y * rows + row).astype(f32) + 0.5) / float(ny * rows)
    coriolis = jnp.sin(math.pi * latitude - 0.5 * math.pi)

    def density(t, s, wet):
        return wet * (-0.2 * t + 0.8 * s - 0.05 * t * t + 0.03 * t * s)

    beside_wet = jnp.where(spot < 3, count_beside[:, cols - 1:cols], count_beside[:, 0:1]) > level_of
    rho_beside = density(lon_both[0], lon_both[1], beside_wet.astype(f32))
    total_beside = rho_beside
    step = 1
    while step < nlev:
        total_beside = total_beside + jnp.where(owner >= step, right(total_beside, wide * step), 0.0)
        step *= 2
    lon_both[4] = thickness * (total_beside - 0.5 * rho_beside)
    least_lon = jnp.minimum(count_here, following(count_here, count_beside))

    def momentum_level(k, slot, carry):
        above, sum_u, sum_v, star_u, star_v = carry
        level = k.astype(f32)
        wet_full = (crow[...] > level).astype(f32)
        wet = (crow[SUB:top, :] > level).astype(f32)
        rho = density(ext[0, k], ext[1, k], wet_full)
        above = above + rho
        pressure = thickness * (above - 0.5 * rho)
        pressure_h = beside(4, k)
        pbuf[slot] = pressure
        p = pbuf[slot, SUB:top, :]
        grad_lon = 0.5 * (following(p, pressure_h) - right(jnp.where(lane == cols - 1, pressure_h, p), 1))
        grad_lat = 0.5 * (pbuf[slot, SUB + 1:top + 1, :] - pbuf[slot, SUB - 1:top - 1, :])
        u = ext[2, k, SUB:top, :]
        v = ext[3, k, SUB:top, :]
        s_lon = jnp.where(least_lon > level, 0.5 * (u + following(u, beside(2, k))), 0.0)
        s_south = lat_speed(k, SUB, SUB)
        s_north = lat_speed(k, top - SUB, SUB)
        speed_lon[k] = s_lon
        speed_lat[0, k] = s_south
        speed_lat[1, k] = s_north
        accel_u = wet * (coriolis * v - advect(2, k, s_lon, s_south, s_north, 2 * slot) - grad_lon)
        accel_v = wet * (-advect(3, k, s_lon, s_south, s_north, 2 * slot + 1) - coriolis * u - grad_lat)
        u_star = wet * u + tracer_step * accel_u
        v_star = wet * v + tracer_step * accel_v
        out[2, k] = u_star
        out[3, k] = v_star
        return above, sum_u + accel_u, sum_v + accel_v, star_u + u_star, star_v + v_star

    def momentum(i, carry):
        for slot in range(2):
            carry = momentum_level(2 * i + slot, slot, carry)
        return carry

    zero = jnp.zeros((rows, cols), f32)
    _, sum_u, sum_v, star_u, star_v = lax.fori_loop(
        0, half, momentum, (jnp.zeros((full, cols), f32), zero, zero, zero, zero))
    per_depth = thickness / jnp.maximum(thickness * count_here, thickness)
    sf[0, 0, SUB:top, :] = sum_u * per_depth
    sf[1, 0, SUB:top, :] = sum_v * per_depth
    mean_star_u = star_u * per_depth
    mean_star_v = star_v * per_depth
    force_lon_pair.start()

    def store(q, k0, k1, sem):
        part = pltpu.make_async_copy(out.at[q:q + 2, k0:k1], out_hbm.at[q:q + 2, k0:k1], store_sem.at[sem])
        part.start()
        return part

    stores = [store(2, 0, nlev, 0)]

    def tracers(i, carry):
        for slot in range(2):
            k = 2 * i + slot
            wet = (crow[SUB:top, :] > k.astype(f32)).astype(f32)
            for q in range(2):
                change = advect(q, k, speed_lon[k], speed_lat[0, k], speed_lat[1, k], 2 * slot + q)
                out[q, k] = wet * (ext[q, k, SUB:top, :] - tracer_step * change)
        return carry

    mid = half // 2
    lax.fori_loop(0, mid, tracers, 0)
    force_lon_pair.wait_recv()
    close_lon(sf, sf_lon, 2)
    stage_north(sf, sf_north, (-1.0, -1.0))
    force_lat_pair.start()
    stores.append(store(0, 0, 2 * mid, 1))
    lax.fori_loop(mid, half, tracers, 0)
    stores.append(store(0, 2 * mid, nlev, 2))
    surf_lat.wait_recv()
    force_lat_pair.wait_recv()

    def slope_lon(c, h):
        up_c = left(jnp.where(lane_full == 0, h, c), 1)
        up_h = left(jnp.where(lane_full == 0, c, h), 1)
        down_c = right(jnp.where(lane_full == cols - 1, h, c), 1)
        down_h = right(jnp.where(lane_full == cols - 1, c, h), 1)
        return 0.5 * (up_c - down_c), 0.5 * (up_h - down_h)

    def slope_lat(c, h):
        return tuple(0.5 * (pltpu.roll(a, full - 1, axis=0) - pltpu.roll(a, 1, axis=0)) for a in (c, h))

    both = (0, 1)
    height = [sa[0, i] for i in both]
    mean_u = [sa[1, i] for i in both]
    mean_v = [sa[2, i] for i in both]
    depth = [thickness * sa[3, i] for i in both]
    sea = [(sa[3, i] > 0.0).astype(f32) for i in both]
    for _ in range(NSUB):
        dx = slope_lon(*[depth[i] * mean_u[i] for i in both])
        dy = slope_lat(*[depth[i] * mean_v[i] for i in both])
        height = [sea[i] * (height[i] - surface_step * (dx[i] + dy[i])) for i in both]
        dx = slope_lon(*height)
        dy = slope_lat(*height)
        mean_u = [sea[i] * (mean_u[i] + surface_step * (sf[0, i] - dx[i])) for i in both]
        mean_v = [sea[i] * (mean_v[i] + surface_step * (sf[1, i] - dy[i])) for i in both]
    surf_out[0] = height[0][SUB:top]
    surf_out[1] = mean_u[0][SUB:top]
    surf_out[2] = mean_v[0][SUB:top]
    gain[0] = zero
    gain[1] = zero
    gain[2] = mean_u[0][SUB:top] - mean_star_u
    gain[3] = mean_v[0][SUB:top] - mean_star_v
    for part in stores:
        part.wait()

    for pair in (surf_lon, level_lon, level_lat, surf_lat, force_lon_pair, force_lat_pair):
        pair.wait_send()


def on_device(nx, ny, ocean_state, surface_state, column_levels):
    _, nlev, rows, cols = ocean_state.shape
    if cols % 128 or nlev * 8 > cols or nlev % 4 or rows % SUB or rows < 3 * SUB or DEEP > SUB or nx % 2:
        raise ValueError("tile shape")
    full = rows + 2 * SUB
    vmem = pltpu.VMEM
    stars, gain, surface_next = pl.pallas_call(
        functools.partial(kernel, nx, ny),
        out_shape=(jax.ShapeDtypeStruct(ocean_state.shape, f32), jax.ShapeDtypeStruct((4, rows, cols), f32),
                   jax.ShapeDtypeStruct(surface_state.shape, f32)),
        in_specs=[pl.BlockSpec(memory_space=pltpu.HBM)] * 3,
        out_specs=(pl.BlockSpec(memory_space=pl.ANY), pl.BlockSpec(memory_space=vmem), pl.BlockSpec(memory_space=vmem)),
        scratch_shapes=[
            vmem((4, nlev, full, cols), f32),
            vmem((4, rows, cols), f32),
            vmem((2, 4, rows, cols), f32),
            vmem((2, 2 * nlev + 1, SUB, cols), f32),
            vmem((2, 2 * nlev + 1, SUB, cols), f32),
            vmem((4, 2, full, cols), f32),
            vmem((2, 2, full, cols), f32),
            vmem((2, 4, rows, cols), f32),
            vmem((2, 2, rows, cols), f32),
            vmem((4, 2, SUB, cols), f32),
            vmem((2, 2, SUB, cols), f32),
            vmem((4, rows, cols), f32),
            vmem((4, nlev, cols), f32),
            vmem((nlev, rows, cols), f32),
            vmem((2, nlev, SUB, cols), f32),
            vmem((2, full, cols), f32),
            vmem((4, full, cols), f32),
            vmem((4, nlev, rows - 2 * SUB, cols), f32),
            vmem((4, nlev, rows, cols), f32),
            vmem((rows, cols), jnp.int32),
            vmem((full, cols), f32),
            vmem((5, rows, cols), f32),
            pltpu.SemaphoreType.DMA((3,)),
            pltpu.SemaphoreType.DMA((3,)),
            pltpu.SemaphoreType.DMA((12,)),
            pltpu.SemaphoreType.DMA((12,)),
        ],
        compiler_params=pltpu.CompilerParams(collective_id=0, has_side_effects=True),
    )(ocean_state, surface_state, column_levels)
    level = lax.broadcasted_iota(jnp.int32, stars.shape, 1)
    return jnp.where(level < column_levels, stars + gain[:, None], 0.0), surface_next


def solution(mesh):
    return jax.shard_map(
        functools.partial(on_device, mesh.shape["lon"], mesh.shape["lat"]),
        mesh=mesh,
        in_specs=(P(None, None, "lat", "lon"), P(None, "lat", "lon"), P("lat", "lon")),
        out_specs=(P(None, None, "lat", "lon"), P(None, "lat", "lon")),
        check_vma=False,
    )
```

```python
import functools
import math

import jax
import jax.numpy as jnp
from jax import lax
from jax.experimental import pallas as pl
from jax.experimental.pallas import tpu as pltpu
from jax.sharding import PartitionSpec as P

NSUB = 4
DEEP = 2 * NSUB
SUB = 8
epsilon = 1e-06
tracer_step = 0.1
surface_step = 1.2
f32 = jnp.float32


def face_flux(s, q0, q1, dm2, dm1, d0, dp1, dp2):
    pos = s >= 0.0
    third = jnp.abs(s) * (1.0 / 3.0)
    c = jnp.where(pos, q0, q1)
    d1 = jnp.where(pos, dm2, dp2)
    d2 = jnp.where(pos, dm1, dp1)
    d3 = d0
    d4 = jnp.where(pos, dp1, dm1)
    rest2 = ((39.0 / 64.0) * d2) * d2 + 0.75 * epsilon
    rest3 = ((39.0 / 64.0) * d3) * d3 + 0.75 * epsilon
    g1 = d1 - (11.0 / 8.0) * d2
    g2 = d2 - (5.0 / 8.0) * d3
    g3 = d4 - (11.0 / 8.0) * d3
    s1 = g1 * g1 + rest2
    s2 = g2 * g2 + rest3
    s3 = g3 * g3 + rest3
    p23 = s2 * s3
    p13 = s1 * s3
    p12 = s1 * s2
    w1 = (p23 * (1.0 / 3.0)) * p23
    w2 = p13 * p13
    w3 = p12 * p12
    twice = d3 + d3
    top = w1 * (2.5 * d2 - d1) + w2 * (d2 + twice) + w3 * (twice - 0.5 * d4)
    total = (w1 + w2) + (w2 + w3)
    return s * c + third * (top * pl.reciprocal(total, approx=True))


def left(x, n):
    return pltpu.roll(x, x.shape[-1] - n, axis=x.ndim - 1)


def right(x, n):
    return pltpu.roll(x, n, axis=x.ndim - 1)


def kernel(nx, ny, ocean, surface, levels_in, out_hbm, gain, surf_out, ext, lon_own, lon_in, lat_out, lat_in, sa, sf,
           sa_lon, sf_lon, sa_north, sf_north, extra_lon, extra_lat, speed_lon, speed_lat, pbuf, fbuf,
           flat, out, counts, crow, lon_both, local_sem, store_sem, send_sem, recv_sem):
    nlev, rows, cols = ocean.shape[1], ocean.shape[2], ocean.shape[3]
    top = SUB + rows
    full = top + SUB
    thickness = 1.0 / nlev
    wide = 8
    x = lax.axis_index("lon")
    y = lax.axis_index("lat")
    at_north = y == ny - 1
    east = {"lon": lax.rem(x + 1, nx), "lat": y}
    west = {"lon": lax.rem(x + nx - 1, nx), "lat": y}
    north = {"lon": jnp.where(at_north, nx - 1 - x, x), "lat": jnp.where(at_north, y, y + 1)}
    south = {"lon": x, "lat": jnp.maximum(y - 1, 0)}
    fold = jnp.where(at_north, 1, 0)
    far_row = pl.multiple_of(fold * top, SUB)

    load = pltpu.make_async_copy(ocean, ext.at[:, :, SUB:top, :], local_sem.at[0])
    load_surface = pltpu.make_async_copy(surface, sa.at[0:3, 0, SUB:top, :], local_sem.at[1])
    load_counts = pltpu.make_async_copy(levels_in, counts, local_sem.at[2])
    load.start()
    load_surface.start()
    load_counts.start()

    @pl.when(y == 0)
    def _():
        sa[:, :, 0:SUB, :] = jnp.zeros((4, 2, SUB, cols), f32)
        sf[:, :, 0:SUB, :] = jnp.zeros((2, 2, SUB, cols), f32)
        lat_in[0] = jnp.zeros(lat_in.shape[1:], f32)

    barrier = pltpu.get_barrier_semaphore()
    for target in (east, west, north):
        pl.semaphore_signal(barrier, inc=1, device_id=target, device_id_type=pl.DeviceIdType.MESH)

    @pl.when(y > 0)
    def _():
        pl.semaphore_signal(barrier, inc=1, device_id=south, device_id_type=pl.DeviceIdType.MESH)

    def remote(src, dst, send, recv, target):
        return pltpu.make_async_remote_copy(
            src_ref=src, dst_ref=dst, send_sem=send_sem.at[send], recv_sem=recv_sem.at[recv],
            device_id=target, device_id_type=pl.DeviceIdType.MESH)

    class LonPair:
        def __init__(self, src, dst, base):
            self.go_east = remote(src, dst.at[0], base, base, east)
            self.go_west = remote(src, dst.at[1], base + 1, base + 1, west)

        def start(self):
            self.go_east.start()
            self.go_west.start()

        def wait_recv(self):
            self.go_east.wait_recv()
            self.go_west.wait_recv()

        def wait_send(self):
            self.go_east.wait_send()
            self.go_west.wait_send()

    class LatPair:
        def __init__(self, north_src, north_dst, south_src, dst_south, dst_north, base):
            self.go_north = remote(north_src, north_dst, base, base + fold, north)
            self.go_south = remote(south_src, dst_north, base + 1, base + 1, south)
            self.from_south = remote(north_src, dst_south, base, base, south)

        def start(self):
            self.go_north.start()

            @pl.when(y > 0)
            def _():
                self.go_south.start()

        def wait_recv(self):
            self.go_south.wait_recv()

            @pl.when(y > 0)
            def _():
                self.from_south.wait_recv()

        def wait_send(self):
            self.go_north.wait_send()

            @pl.when(y > 0)
            def _():
                self.go_south.wait_send()

    surf_lon = LonPair(sa.at[:, 0, SUB:top, :], sa_lon, 0)
    level_lon = LonPair(lon_own, lon_in, 2)
    force_lon_pair = LonPair(sf.at[:, 0, SUB:top, :], sf_lon, 4)
    level_lat = LatPair(lat_out.at[0], lat_in.at[fold], lat_out.at[1], lat_in.at[0], lat_in.at[1], 6)
    surf_lat = LatPair(sa_north, sa.at[:, :, pl.ds(far_row, SUB), :], sa.at[:, :, SUB:2 * SUB, :],
                       sa.at[:, :, 0:SUB, :], sa.at[:, :, top:full, :], 8)
    force_lat_pair = LatPair(sf_north, sf.at[:, :, pl.ds(far_row, SUB), :], sf.at[:, :, SUB:2 * SUB, :],
                             sf.at[:, :, 0:SUB, :], sf.at[:, :, top:full, :], 10)

    lane = lax.broadcasted_iota(jnp.int32, (rows, cols), 1)
    lane_full = lax.broadcasted_iota(jnp.int32, (full, cols), 1)
    spot = lane % wide
    owner = lane // wide
    sub8 = lax.broadcasted_iota(jnp.int32, (SUB, cols), 0)

    def mirrored(block):
        for axis, length in ((0, SUB), (1, cols)):
            at = lax.broadcasted_iota(jnp.int32, block.shape, axis)
            size = block.shape[axis]
            step = 1
            while step < length:
                up = pltpu.roll(block, step, axis=axis)
                down = pltpu.roll(block, size - step, axis=axis)
                block = jnp.where((at // step) % 2 == 1, up, down)
                step *= 2
        return block

    load.wait()
    half = nlev // 2
    for q in range(4):
        for h in range(half):
            n0 = ext[q, 2 * h, top - SUB:top, :]
            n1 = ext[q, 2 * h + 1, top - SUB:top, :]
            lat_out[0, q * half + h] = jnp.where(sub8 >= 4, n0, pltpu.roll(n1, 4, axis=0))
            s0 = ext[q, 2 * h, SUB:2 * SUB, :]
            s1 = ext[q, 2 * h + 1, SUB:2 * SUB, :]
            lat_out[1, q * half + h] = jnp.where(sub8 < 4, s0, pltpu.roll(s1, 4, axis=0))

    load_surface.wait()
    load_counts.wait()
    sa[3, 0, SUB:top, :] = counts[...].astype(f32)
    crow[SUB:top, :] = sa[3, 0, SUB:top, :]
    lat_out[0, 4 * half] = crow[top - SUB:top, :]
    lat_out[1, 4 * half] = crow[SUB:2 * SUB, :]

    @pl.when(at_north)
    def _():
        lat_out[0, 4 * half] = mirrored(lat_out[0, 4 * half])
        for q in range(4):
            sign = 1.0 if q < 2 else -1.0
            block = lat_out[0, q * half:(q + 1) * half].reshape(half * SUB, cols)
            lat_out[0, q * half:(q + 1) * half] = (sign * mirrored(block)).reshape(half, SUB, cols)

    pl.semaphore_wait(barrier, 3 + jnp.where(y > 0, 1, 0))
    level_lat.start()
    surf_lon.start()

    for q in range(4):
        pack = jnp.zeros((rows, cols), f32)
        for k in range(nlev):
            pack = jnp.where(owner == k, right(ext[q, k, SUB:top, :], wide * k + 3), pack)
        lon_own[q] = pack
    level_lon.start()

    def close_lon(fields, arrived, count):
        for f in range(count):
            fields[f, 1, SUB:top, :] = jnp.where(lane < cols // 2, arrived[1, f], arrived[0, f])

    def stage_north(fields, staged, signs):
        count = len(signs)
        for f in range(count):
            for part in range(2):
                staged[f, part] = fields[f, part, top - SUB:top, :]

        @pl.when(at_north)
        def _():
            for f in range(count):
                block = staged[f].reshape(2 * SUB, cols)
                staged[f] = (signs[f] * mirrored(block)).reshape(2, SUB, cols)

    def face_rows(q, k, s, first, count):
        start = first - 2 + jnp.minimum(k, 0)
        cell = [ext[q, k, pl.ds(start + i, count), :] for i in range(6)]
        return face_flux(s, cell[2], cell[3], *[cell[i + 1] - cell[i] for i in range(5)])

    def lat_speed(k, first, count):
        least = jnp.minimum(crow[first:first + count, :], crow[first + 1:first + 1 + count, :])
        speed = 0.5 * (ext[3, k, first:first + count, :] + ext[3, k, first + 1:first + 1 + count, :])
        return jnp.where(least > k.astype(f32), speed, 0.0)

    inner, inner_count = 2 * SUB, rows - 2 * SUB

    def inner_faces(i, carry):
        for k in (2 * i, 2 * i + 1):
            s = lat_speed(k, inner, inner_count)
            for q in range(4):
                flat[q, k] = face_rows(q, k, s, inner, inner_count)
        return carry

    lax.fori_loop(0, half, inner_faces, 0)

    surf_lon.wait_recv()
    close_lon(sa, sa_lon, 4)
    stage_north(sa, sa_north, (1.0, -1.0, -1.0, 1.0))
    surf_lat.start()

    level_lon.wait_recv()

    def lon_pack(q):
        return jnp.where(spot < 3, lon_in[0, q], lon_own[q])

    count_here = crow[SUB:top, :]
    count_beside = sa[3, 1, SUB:top, :]
    level_of = owner.astype(f32)
    for q in range(4):
        lon_both[q] = jnp.where(spot < 3, lon_in[0, q], lon_in[1, q])
    edge_wet = ((count_beside[:, cols - 1:cols] > level_of) & (count_here[:, 0:1] > level_of)).astype(f32)
    pack_u = lon_pack(2)
    edge_speed = 0.5 * (pack_u + left(pack_u, 1)) * edge_wet
    for q in range(4):
        pack = lon_pack(q)
        d = left(pack, 1) - pack
        extra_lon[q] = face_flux(edge_speed, pack, left(pack, 1), right(d, 2), right(d, 1), d, left(d, 1),
                                 left(d, 2))

    def beside(q, k):
        return pltpu.roll(lon_both[q], cols - 3 - wide * k, axis=1)

    def following(c, h):
        return left(jnp.where(lane == 0, h, c), 1)

    def advect_lon(q, k, s_lon):
        c = ext[q, k, SUB:top, :]
        h = beside(q, k)
        c1 = following(c, h)
        d = c1 - c
        dh = following(h, c) - h
        flux = face_flux(
            s_lon, c, c1,
            right(jnp.where(lane >= cols - 2, dh, d), 2),
            right(jnp.where(lane >= cols - 1, dh, d), 1),
            d,
            left(jnp.where(lane < 1, dh, d), 1),
            left(jnp.where(lane < 2, dh, d), 2))
        edge = pltpu.roll(extra_lon[q], cols - 2 - wide * k, axis=1)
        return flux - jnp.where(lane == 0, edge, right(flux, 1))

    least_lon = jnp.minimum(count_here, following(count_here, count_beside))

    def velocity_lon(i, carry):
        for k in (2 * i, 2 * i + 1):
            u = ext[2, k, SUB:top, :]
            s_lon = jnp.where(least_lon > k.astype(f32), 0.5 * (u + following(u, beside(2, k))), 0.0)
            speed_lon[k] = s_lon
            out[2, k] = advect_lon(2, k, s_lon)
            out[3, k] = advect_lon(3, k, s_lon)
        return carry

    lax.fori_loop(0, half, velocity_lon, 0)

    level_lat.wait_recv()
    crow[0:SUB, :] = lat_in[0, 4 * half]
    crow[top:full, :] = lat_in[1, 4 * half]

    for q in range(4):
        for h in range(half):
            for side, place in ((0, 0), (1, top)):
                block = lat_in[side, q * half + h]
                ext[q, 2 * h, place:place + SUB, :] = block
                ext[q, 2 * h + 1, place:place + SUB, :] = pltpu.roll(block, 4, axis=0)

    level_row = lax.broadcasted_iota(jnp.int32, (nlev, cols), 0).astype(f32)
    row_wet = ((crow[SUB - 1:SUB, :] > level_row) & (crow[SUB:SUB + 1, :] > level_row)).astype(f32)
    row_speed = 0.5 * (ext[3, :, SUB - 1, :] + ext[3, :, SUB, :]) * row_wet
    for q in range(4):
        cell = [ext[q, :, SUB - 3 + i, :] for i in range(6)]
        d = [cell[i + 1] - cell[i] for i in range(5)]
        extra_lat[q] = face_flux(row_speed, cell[2], cell[3], *d)

    def advect_lat(q, k, s_south, s_north, slot):
        fbuf[slot, SUB - 1:SUB, :] = extra_lat[q, pl.ds(k, 1), :]
        fbuf[slot, SUB:2 * SUB, :] = face_rows(q, k, s_south, SUB, SUB)
        fbuf[slot, inner:top - SUB, :] = flat[q, k]
        fbuf[slot, top - SUB:top, :] = face_rows(q, k, s_north, top - SUB, SUB)
        return fbuf[slot, SUB:top, :] - fbuf[slot, SUB - 1:top - 1, :]

    row = lax.broadcasted_iota(jnp.int32, (rows, cols), 0)
    latitude = ((y * rows + row).astype(f32) + 0.5) / float(ny * rows)
    coriolis = jnp.sin(math.pi * latitude - 0.5 * math.pi)

    def density(t, s, wet):
        return wet * (-0.2 * t + 0.8 * s - 0.05 * t * t + 0.03 * t * s)

    beside_wet = jnp.where(spot < 3, count_beside[:, cols - 1:cols], count_beside[:, 0:1]) > level_of
    rho_beside = density(lon_both[0], lon_both[1], beside_wet.astype(f32))
    total_beside = rho_beside
    step = 1
    while step < nlev:
        total_beside = total_beside + jnp.where(owner >= step, right(total_beside, wide * step), 0.0)
        step *= 2
    lon_both[4] = thickness * (total_beside - 0.5 * rho_beside)
    def momentum_level(k, slot, carry):
        above, sum_u, sum_v, star_u, star_v = carry
        level = k.astype(f32)
        wet_full = (crow[...] > level).astype(f32)
        wet = (crow[SUB:top, :] > level).astype(f32)
        rho = density(ext[0, k], ext[1, k], wet_full)
        above = above + rho
        pressure = thickness * (above - 0.5 * rho)
        pressure_h = beside(4, k)
        pbuf[slot] = pressure
        p = pbuf[slot, SUB:top, :]
        grad_lon = 0.5 * (following(p, pressure_h) - right(jnp.where(lane == cols - 1, pressure_h, p), 1))
        grad_lat = 0.5 * (pbuf[slot, SUB + 1:top + 1, :] - pbuf[slot, SUB - 1:top - 1, :])
        u = ext[2, k, SUB:top, :]
        v = ext[3, k, SUB:top, :]
        s_south = lat_speed(k, SUB, SUB)
        s_north = lat_speed(k, top - SUB, SUB)
        speed_lat[0, k] = s_south
        speed_lat[1, k] = s_north
        accel_u = wet * (coriolis * v - (out[2, k] + advect_lat(2, k, s_south, s_north, 2 * slot)) - grad_lon)
        accel_v = wet * (-(out[3, k] + advect_lat(3, k, s_south, s_north, 2 * slot + 1)) - coriolis * u - grad_lat)
        u_star = wet * u + tracer_step * accel_u
        v_star = wet * v + tracer_step * accel_v
        out[2, k] = u_star
        out[3, k] = v_star
        return above, sum_u + accel_u, sum_v + accel_v, star_u + u_star, star_v + v_star

    def momentum(i, carry):
        for slot in range(2):
            carry = momentum_level(2 * i + slot, slot, carry)
        return carry

    zero = jnp.zeros((rows, cols), f32)
    _, sum_u, sum_v, star_u, star_v = lax.fori_loop(
        0, half, momentum, (jnp.zeros((full, cols), f32), zero, zero, zero, zero))
    per_depth = thickness / jnp.maximum(thickness * count_here, thickness)
    sf[0, 0, SUB:top, :] = sum_u * per_depth
    sf[1, 0, SUB:top, :] = sum_v * per_depth
    mean_star_u = star_u * per_depth
    mean_star_v = star_v * per_depth
    force_lon_pair.start()

    def store(q, k0, k1, sem):
        part = pltpu.make_async_copy(out.at[q:q + 2, k0:k1], out_hbm.at[q:q + 2, k0:k1], store_sem.at[sem])
        part.start()
        return part

    stores = [store(2, 0, nlev, 0)]

    def tracers(i, carry):
        for slot in range(2):
            k = 2 * i + slot
            wet = (crow[SUB:top, :] > k.astype(f32)).astype(f32)
            for q in range(2):
                change = advect_lon(q, k, speed_lon[k]) + advect_lat(
                    q, k, speed_lat[0, k], speed_lat[1, k], 2 * slot + q)
                out[q, k] = wet * (ext[q, k, SUB:top, :] - tracer_step * change)
        return carry

    mid = half // 2
    lax.fori_loop(0, mid, tracers, 0)
    force_lon_pair.wait_recv()
    close_lon(sf, sf_lon, 2)
    stage_north(sf, sf_north, (-1.0, -1.0))
    force_lat_pair.start()
    stores.append(store(0, 0, 2 * mid, 1))
    lax.fori_loop(mid, half, tracers, 0)
    stores.append(store(0, 2 * mid, nlev, 2))
    surf_lat.wait_recv()
    force_lat_pair.wait_recv()

    def slope_lon(c, h):
        up_c = left(jnp.where(lane_full == 0, h, c), 1)
        up_h = left(jnp.where(lane_full == 0, c, h), 1)
        down_c = right(jnp.where(lane_full == cols - 1, h, c), 1)
        down_h = right(jnp.where(lane_full == cols - 1, c, h), 1)
        return 0.5 * (up_c - down_c), 0.5 * (up_h - down_h)

    def slope_lat(c, h):
        return tuple(0.5 * (pltpu.roll(a, full - 1, axis=0) - pltpu.roll(a, 1, axis=0)) for a in (c, h))

    both = (0, 1)
    height = [sa[0, i] for i in both]
    mean_u = [sa[1, i] for i in both]
    mean_v = [sa[2, i] for i in both]
    depth = [thickness * sa[3, i] for i in both]
    sea = [(sa[3, i] > 0.0).astype(f32) for i in both]
    for _ in range(NSUB):
        dx = slope_lon(*[depth[i] * mean_u[i] for i in both])
        dy = slope_lat(*[depth[i] * mean_v[i] for i in both])
        height = [sea[i] * (height[i] - surface_step * (dx[i] + dy[i])) for i in both]
        dx = slope_lon(*height)
        dy = slope_lat(*height)
        mean_u = [sea[i] * (mean_u[i] + surface_step * (sf[0, i] - dx[i])) for i in both]
        mean_v = [sea[i] * (mean_v[i] + surface_step * (sf[1, i] - dy[i])) for i in both]
    surf_out[0] = height[0][SUB:top]
    surf_out[1] = mean_u[0][SUB:top]
    surf_out[2] = mean_v[0][SUB:top]
    gain[0] = mean_u[0][SUB:top] - mean_star_u
    gain[1] = mean_v[0][SUB:top] - mean_star_v
    for part in stores:
        part.wait()

    for pair in (surf_lon, level_lon, level_lat, surf_lat, force_lon_pair, force_lat_pair):
        pair.wait_send()


def finish_kernel(stars, gain, surface, counts, out, surf_out, buf, gain_buf, surf_buf, count_buf, in_sem, out_sem):
    nlev = stars.shape[1]
    half = nlev // 2
    places = [(q, h) for q in (2, 3, 0, 1) for h in range(2)]
    copy = pltpu.make_async_copy
    small = [copy(gain, gain_buf, in_sem.at[8]), copy(counts, count_buf, in_sem.at[9]),
             copy(surface, surf_buf, in_sem.at[10])]
    loads = [copy(stars.at[q, h * half:(h + 1) * half], buf.at[q, h * half:(h + 1) * half], in_sem.at[i])
             for i, (q, h) in enumerate(places)]
    stores = [copy(buf.at[q, h * half:(h + 1) * half], out.at[q, h * half:(h + 1) * half], out_sem.at[i])
              for i, (q, h) in enumerate(places)]
    last = copy(surf_buf, surf_out, out_sem.at[8])
    for part in small + loads:
        part.start()
    for part in small:
        part.wait()
    last.start()
    for i, (q, h) in enumerate(places):
        loads[i].wait()
        if q >= 2:
            for k in range(h * half, (h + 1) * half):
                buf[q, k] = jnp.where(count_buf[...] > k, buf[q, k] + gain_buf[q - 2], 0.0)
        stores[i].start()
    for part in stores + [last]:
        part.wait()


def on_device(nx, ny, ocean_state, surface_state, column_levels):
    _, nlev, rows, cols = ocean_state.shape
    if cols % 128 or nlev * 8 > cols or nlev % 4 or rows % SUB or rows < 3 * SUB or DEEP > SUB or nx % 2:
        raise ValueError("tile shape")
    full = rows + 2 * SUB
    vmem = pltpu.VMEM
    stars, gain, surface_next = pl.pallas_call(
        functools.partial(kernel, nx, ny),
        out_shape=(jax.ShapeDtypeStruct(ocean_state.shape, f32), jax.ShapeDtypeStruct((2, rows, cols), f32),
                   jax.ShapeDtypeStruct(surface_state.shape, f32)),
        in_specs=[pl.BlockSpec(memory_space=pltpu.HBM)] * 3,
        out_specs=(pl.BlockSpec(memory_space=pl.ANY), pl.BlockSpec(memory_space=vmem), pl.BlockSpec(memory_space=vmem)),
        scratch_shapes=[
            vmem((4, nlev, full, cols), f32),
            vmem((4, rows, cols), f32),
            vmem((2, 4, rows, cols), f32),
            vmem((2, 2 * nlev + 1, SUB, cols), f32),
            vmem((2, 2 * nlev + 1, SUB, cols), f32),
            vmem((4, 2, full, cols), f32),
            vmem((2, 2, full, cols), f32),
            vmem((2, 4, rows, cols), f32),
            vmem((2, 2, rows, cols), f32),
            vmem((4, 2, SUB, cols), f32),
            vmem((2, 2, SUB, cols), f32),
            vmem((4, rows, cols), f32),
            vmem((4, nlev, cols), f32),
            vmem((nlev, rows, cols), f32),
            vmem((2, nlev, SUB, cols), f32),
            vmem((2, full, cols), f32),
            vmem((4, full, cols), f32),
            vmem((4, nlev, rows - 2 * SUB, cols), f32),
            vmem((4, nlev, rows, cols), f32),
            vmem((rows, cols), jnp.int32),
            vmem((full, cols), f32),
            vmem((5, rows, cols), f32),
            pltpu.SemaphoreType.DMA((3,)),
            pltpu.SemaphoreType.DMA((3,)),
            pltpu.SemaphoreType.DMA((12,)),
            pltpu.SemaphoreType.DMA((12,)),
        ],
        compiler_params=pltpu.CompilerParams(collective_id=0, has_side_effects=True),
    )(ocean_state, surface_state, column_levels)
    parts = 8
    return pl.pallas_call(
        finish_kernel,
        out_shape=(jax.ShapeDtypeStruct(ocean_state.shape, f32), jax.ShapeDtypeStruct(surface_state.shape, f32)),
        in_specs=[pl.BlockSpec(memory_space=pl.ANY)] * 4,
        out_specs=(pl.BlockSpec(memory_space=pl.ANY),) * 2,
        scratch_shapes=[
            vmem(ocean_state.shape, f32),
            vmem((2, rows, cols), f32),
            vmem(surface_state.shape, f32),
            vmem((rows, cols), jnp.int32),
            pltpu.SemaphoreType.DMA((parts + 3,)),
            pltpu.SemaphoreType.DMA((parts + 1,)),
        ],
    )(stars, gain, surface_next, column_levels)


def solution(mesh):
    return jax.shard_map(
        functools.partial(on_device, mesh.shape["lon"], mesh.shape["lat"]),
        mesh=mesh,
        in_specs=(P(None, None, "lat", "lon"), P(None, "lat", "lon"), P("lat", "lon")),
        out_specs=(P(None, None, "lat", "lon"), P(None, "lat", "lon")),
        check_vma=False,
    )
```

```python
import functools
import math

import jax
import jax.numpy as jnp
from jax import lax
from jax.experimental import pallas as pl
from jax.experimental.pallas import tpu as pltpu
from jax.sharding import PartitionSpec as P

NSUB = 4
DEEP = 2 * NSUB
SUB = 8
epsilon = 1e-06
tracer_step = 0.1
surface_step = 1.2
f32 = jnp.float32


def face_flux(s, q0, q1, dm2, dm1, d0, dp1, dp2):
    pos = s >= 0.0
    third = jnp.abs(s) * (1.0 / 3.0)
    c = jnp.where(pos, q0, q1)
    d1 = jnp.where(pos, dm2, dp2)
    d2 = jnp.where(pos, dm1, dp1)
    d3 = d0
    d4 = jnp.where(pos, dp1, dm1)
    rest2 = ((39.0 / 64.0) * d2) * d2 + 0.75 * epsilon
    rest3 = ((39.0 / 64.0) * d3) * d3 + 0.75 * epsilon
    g1 = d1 - (11.0 / 8.0) * d2
    g2 = d2 - (5.0 / 8.0) * d3
    g3 = d4 - (11.0 / 8.0) * d3
    s1 = g1 * g1 + rest2
    s2 = g2 * g2 + rest3
    s3 = g3 * g3 + rest3
    p23 = s2 * s3
    p13 = s1 * s3
    p12 = s1 * s2
    w1 = (p23 * (1.0 / 3.0)) * p23
    w2 = p13 * p13
    w3 = p12 * p12
    twice = d3 + d3
    top = w1 * (2.5 * d2 - d1) + w2 * (d2 + twice) + w3 * (twice - 0.5 * d4)
    total = (w1 + w2) + (w2 + w3)
    return s * c + third * (top * pl.reciprocal(total, approx=True))


def left(x, n):
    return pltpu.roll(x, x.shape[-1] - n, axis=x.ndim - 1)


def right(x, n):
    return pltpu.roll(x, n, axis=x.ndim - 1)


def kernel(nx, ny, ocean, surface, levels_in, out_hbm, gain, surf_out, ext, lon_own, lon_in, lat_out, lat_in, sa, sf,
           sa_lon, sf_lon, sa_north, sf_north, extra_lon, extra_lat, speed_lon, pbuf, fbuf,
           flat, out, counts, crow, lon_both, local_sem, store_sem, send_sem, recv_sem):
    nlev, rows, cols = ocean.shape[1], ocean.shape[2], ocean.shape[3]
    top = SUB + rows
    full = top + SUB
    thickness = 1.0 / nlev
    wide = 8
    x = lax.axis_index("lon")
    y = lax.axis_index("lat")
    at_north = y == ny - 1
    east = {"lon": lax.rem(x + 1, nx), "lat": y}
    west = {"lon": lax.rem(x + nx - 1, nx), "lat": y}
    north = {"lon": jnp.where(at_north, nx - 1 - x, x), "lat": jnp.where(at_north, y, y + 1)}
    south = {"lon": x, "lat": jnp.maximum(y - 1, 0)}
    fold = jnp.where(at_north, 1, 0)
    far_row = pl.multiple_of(fold * top, SUB)

    load = pltpu.make_async_copy(ocean, ext.at[:, :, SUB:top, :], local_sem.at[0])
    load_surface = pltpu.make_async_copy(surface, sa.at[0:3, 0, SUB:top, :], local_sem.at[1])
    load_counts = pltpu.make_async_copy(levels_in, counts, local_sem.at[2])
    load.start()
    load_surface.start()
    load_counts.start()

    @pl.when(y == 0)
    def _():
        sa[:, :, 0:SUB, :] = jnp.zeros((4, 2, SUB, cols), f32)
        sf[:, :, 0:SUB, :] = jnp.zeros((2, 2, SUB, cols), f32)
        lat_in[0] = jnp.zeros(lat_in.shape[1:], f32)

    barrier = pltpu.get_barrier_semaphore()
    for target in (east, west, north):
        pl.semaphore_signal(barrier, inc=1, device_id=target, device_id_type=pl.DeviceIdType.MESH)

    @pl.when(y > 0)
    def _():
        pl.semaphore_signal(barrier, inc=1, device_id=south, device_id_type=pl.DeviceIdType.MESH)

    def remote(src, dst, send, recv, target):
        return pltpu.make_async_remote_copy(
            src_ref=src, dst_ref=dst, send_sem=send_sem.at[send], recv_sem=recv_sem.at[recv],
            device_id=target, device_id_type=pl.DeviceIdType.MESH)

    class LonPair:
        def __init__(self, src, dst, base):
            self.go_east = remote(src, dst.at[0], base, base, east)
            self.go_west = remote(src, dst.at[1], base + 1, base + 1, west)

        def start(self):
            self.go_east.start()
            self.go_west.start()

        def wait_recv(self):
            self.go_east.wait_recv()
            self.go_west.wait_recv()

        def wait_send(self):
            self.go_east.wait_send()
            self.go_west.wait_send()

    class LatPair:
        def __init__(self, north_src, north_dst, south_src, dst_south, dst_north, base):
            self.go_north = remote(north_src, north_dst, base, base + fold, north)
            self.go_south = remote(south_src, dst_north, base + 1, base + 1, south)
            self.from_south = remote(north_src, dst_south, base, base, south)

        def start(self):
            self.go_north.start()

            @pl.when(y > 0)
            def _():
                self.go_south.start()

        def wait_recv(self):
            self.go_south.wait_recv()

            @pl.when(y > 0)
            def _():
                self.from_south.wait_recv()

        def wait_send(self):
            self.go_north.wait_send()

            @pl.when(y > 0)
            def _():
                self.go_south.wait_send()

    surf_lon = LonPair(sa.at[:, 0, SUB:top, :], sa_lon, 0)
    level_lon = LonPair(lon_own, lon_in, 2)
    force_lon_pair = LonPair(sf.at[:, 0, SUB:top, :], sf_lon, 4)
    level_lat = LatPair(lat_out.at[0], lat_in.at[fold], lat_out.at[1], lat_in.at[0], lat_in.at[1], 6)
    surf_lat = LatPair(sa_north, sa.at[:, :, pl.ds(far_row, SUB), :], sa.at[:, :, SUB:2 * SUB, :],
                       sa.at[:, :, 0:SUB, :], sa.at[:, :, top:full, :], 8)
    force_lat_pair = LatPair(sf_north, sf.at[:, :, pl.ds(far_row, SUB), :], sf.at[:, :, SUB:2 * SUB, :],
                             sf.at[:, :, 0:SUB, :], sf.at[:, :, top:full, :], 10)

    lane = lax.broadcasted_iota(jnp.int32, (rows, cols), 1)
    lane_full = lax.broadcasted_iota(jnp.int32, (full, cols), 1)
    spot = lane % wide
    owner = lane // wide
    sub8 = lax.broadcasted_iota(jnp.int32, (SUB, cols), 0)

    def mirrored(block):
        for axis, length in ((0, SUB), (1, cols)):
            at = lax.broadcasted_iota(jnp.int32, block.shape, axis)
            size = block.shape[axis]
            step = 1
            while step < length:
                up = pltpu.roll(block, step, axis=axis)
                down = pltpu.roll(block, size - step, axis=axis)
                block = jnp.where((at // step) % 2 == 1, up, down)
                step *= 2
        return block

    load.wait()
    half = nlev // 2
    for q in range(4):
        for h in range(half):
            n0 = ext[q, 2 * h, top - SUB:top, :]
            n1 = ext[q, 2 * h + 1, top - SUB:top, :]
            lat_out[0, q * half + h] = jnp.where(sub8 >= 4, n0, pltpu.roll(n1, 4, axis=0))
            s0 = ext[q, 2 * h, SUB:2 * SUB, :]
            s1 = ext[q, 2 * h + 1, SUB:2 * SUB, :]
            lat_out[1, q * half + h] = jnp.where(sub8 < 4, s0, pltpu.roll(s1, 4, axis=0))

    load_surface.wait()
    load_counts.wait()
    sa[3, 0, SUB:top, :] = counts[...].astype(f32)
    crow[SUB:top, :] = sa[3, 0, SUB:top, :]
    lat_out[0, 4 * half] = crow[top - SUB:top, :]
    lat_out[1, 4 * half] = crow[SUB:2 * SUB, :]

    @pl.when(at_north)
    def _():
        lat_out[0, 4 * half] = mirrored(lat_out[0, 4 * half])
        for q in range(4):
            sign = 1.0 if q < 2 else -1.0
            block = lat_out[0, q * half:(q + 1) * half].reshape(half * SUB, cols)
            lat_out[0, q * half:(q + 1) * half] = (sign * mirrored(block)).reshape(half, SUB, cols)

    pl.semaphore_wait(barrier, 3 + jnp.where(y > 0, 1, 0))
    level_lat.start()
    surf_lon.start()

    for q in range(4):
        pack = jnp.zeros((rows, cols), f32)
        for k in range(nlev):
            pack = jnp.where(owner == k, right(ext[q, k, SUB:top, :], wide * k + 3), pack)
        lon_own[q] = pack
    level_lon.start()

    def close_lon(fields, arrived, count):
        for f in range(count):
            fields[f, 1, SUB:top, :] = jnp.where(lane < cols // 2, arrived[1, f], arrived[0, f])

    def stage_north(fields, staged, signs):
        count = len(signs)
        for f in range(count):
            for part in range(2):
                staged[f, part] = fields[f, part, top - SUB:top, :]

        @pl.when(at_north)
        def _():
            for f in range(count):
                block = staged[f].reshape(2 * SUB, cols)
                staged[f] = (signs[f] * mirrored(block)).reshape(2, SUB, cols)

    def face_rows(q, k, s, first, count):
        start = first - 2 + jnp.minimum(k, 0)
        cell = [ext[q, k, pl.ds(start + i, count), :] for i in range(6)]
        return face_flux(s, cell[2], cell[3], *[cell[i + 1] - cell[i] for i in range(5)])

    def lat_speed(k, first, count):
        least = jnp.minimum(crow[first:first + count, :], crow[first + 1:first + 1 + count, :])
        speed = 0.5 * (ext[3, k, first:first + count, :] + ext[3, k, first + 1:first + 1 + count, :])
        return jnp.where(least > k.astype(f32), speed, 0.0)

    inner, inner_count = 2 * SUB, rows - 2 * SUB

    def inner_faces(i, carry):
        for k in (2 * i, 2 * i + 1):
            s = lat_speed(k, inner, inner_count)
            for q in (2, 3):
                flat[q - 2, k] = face_rows(q, k, s, inner, inner_count)
        return carry

    lax.fori_loop(0, half, inner_faces, 0)

    surf_lon.wait_recv()
    close_lon(sa, sa_lon, 4)
    stage_north(sa, sa_north, (1.0, -1.0, -1.0, 1.0))
    surf_lat.start()

    level_lon.wait_recv()

    def lon_pack(q):
        return jnp.where(spot < 3, lon_in[0, q], lon_own[q])

    count_here = crow[SUB:top, :]
    count_beside = sa[3, 1, SUB:top, :]
    level_of = owner.astype(f32)
    for q in range(4):
        lon_both[q] = jnp.where(spot < 3, lon_in[0, q], lon_in[1, q])
    edge_wet = ((count_beside[:, cols - 1:cols] > level_of) & (count_here[:, 0:1] > level_of)).astype(f32)
    pack_u = lon_pack(2)
    edge_speed = 0.5 * (pack_u + left(pack_u, 1)) * edge_wet
    for q in range(4):
        pack = lon_pack(q)
        d = left(pack, 1) - pack
        extra_lon[q] = face_flux(edge_speed, pack, left(pack, 1), right(d, 2), right(d, 1), d, left(d, 1),
                                 left(d, 2))

    def beside(q, k):
        return pltpu.roll(lon_both[q], cols - 3 - wide * k, axis=1)

    def following(c, h):
        return left(jnp.where(lane == 0, h, c), 1)

    def advect_lon(q, k, s_lon):
        c = ext[q, k, SUB:top, :]
        h = beside(q, k)
        c1 = following(c, h)
        d = c1 - c
        dh = following(h, c) - h
        flux = face_flux(
            s_lon, c, c1,
            right(jnp.where(lane >= cols - 2, dh, d), 2),
            right(jnp.where(lane >= cols - 1, dh, d), 1),
            d,
            left(jnp.where(lane < 1, dh, d), 1),
            left(jnp.where(lane < 2, dh, d), 2))
        edge = pltpu.roll(extra_lon[q], cols - 2 - wide * k, axis=1)
        return flux - jnp.where(lane == 0, edge, right(flux, 1))

    least_lon = jnp.minimum(count_here, following(count_here, count_beside))

    level_lat.wait_recv()
    crow[0:SUB, :] = lat_in[0, 4 * half]
    crow[top:full, :] = lat_in[1, 4 * half]

    for q in range(4):
        for h in range(half):
            for side, place in ((0, 0), (1, top)):
                block = lat_in[side, q * half + h]
                ext[q, 2 * h, place:place + SUB, :] = block
                ext[q, 2 * h + 1, place:place + SUB, :] = pltpu.roll(block, 4, axis=0)

    level_row = lax.broadcasted_iota(jnp.int32, (nlev, cols), 0).astype(f32)
    row_wet = ((crow[SUB - 1:SUB, :] > level_row) & (crow[SUB:SUB + 1, :] > level_row)).astype(f32)
    row_speed = 0.5 * (ext[3, :, SUB - 1, :] + ext[3, :, SUB, :]) * row_wet
    for q in range(4):
        cell = [ext[q, :, SUB - 3 + i, :] for i in range(6)]
        d = [cell[i + 1] - cell[i] for i in range(5)]
        extra_lat[q] = face_flux(row_speed, cell[2], cell[3], *d)

    def advect_lat(q, k, s_south, s_north, slot):
        fbuf[slot, SUB - 1:SUB, :] = extra_lat[q, pl.ds(k, 1), :]
        fbuf[slot, SUB:2 * SUB, :] = face_rows(q, k, s_south, SUB, SUB)
        fbuf[slot, inner:top - SUB, :] = flat[q - 2, k]
        fbuf[slot, top - SUB:top, :] = face_rows(q, k, s_north, top - SUB, SUB)
        return fbuf[slot, SUB:top, :] - fbuf[slot, SUB - 1:top - 1, :]

    row = lax.broadcasted_iota(jnp.int32, (rows, cols), 0)
    latitude = ((y * rows + row).astype(f32) + 0.5) / float(ny * rows)
    coriolis = jnp.sin(math.pi * latitude - 0.5 * math.pi)

    def density(t, s, wet):
        return wet * (-0.2 * t + 0.8 * s - 0.05 * t * t + 0.03 * t * s)

    beside_wet = jnp.where(spot < 3, count_beside[:, cols - 1:cols], count_beside[:, 0:1]) > level_of
    rho_beside = density(lon_both[0], lon_both[1], beside_wet.astype(f32))
    total_beside = rho_beside
    step = 1
    while step < nlev:
        total_beside = total_beside + jnp.where(owner >= step, right(total_beside, wide * step), 0.0)
        step *= 2
    lon_both[4] = thickness * (total_beside - 0.5 * rho_beside)
    def momentum_level(k, slot, carry):
        above, sum_u, sum_v, star_u, star_v = carry
        level = k.astype(f32)
        wet_full = (crow[...] > level).astype(f32)
        wet = (crow[SUB:top, :] > level).astype(f32)
        rho = density(ext[0, k], ext[1, k], wet_full)
        above = above + rho
        pressure = thickness * (above - 0.5 * rho)
        pressure_h = beside(4, k)
        pbuf[slot] = pressure
        p = pbuf[slot, SUB:top, :]
        grad_lon = 0.5 * (following(p, pressure_h) - right(jnp.where(lane == cols - 1, pressure_h, p), 1))
        grad_lat = 0.5 * (pbuf[slot, SUB + 1:top + 1, :] - pbuf[slot, SUB - 1:top - 1, :])
        u = ext[2, k, SUB:top, :]
        v = ext[3, k, SUB:top, :]
        s_lon = jnp.where(least_lon > level, 0.5 * (u + following(u, beside(2, k))), 0.0)
        speed_lon[k] = s_lon
        s_south = lat_speed(k, SUB, SUB)
        s_north = lat_speed(k, top - SUB, SUB)
        accel_u = wet * (coriolis * v - (advect_lon(2, k, s_lon) + advect_lat(2, k, s_south, s_north, 2 * slot)) - grad_lon)
        accel_v = wet * (-(advect_lon(3, k, s_lon) + advect_lat(3, k, s_south, s_north, 2 * slot + 1)) - coriolis * u - grad_lat)
        u_star = wet * u + tracer_step * accel_u
        v_star = wet * v + tracer_step * accel_v
        out[2, k] = u_star
        out[3, k] = v_star
        return above, sum_u + accel_u, sum_v + accel_v, star_u + u_star, star_v + v_star

    def momentum(i, carry):
        for slot in range(2):
            carry = momentum_level(2 * i + slot, slot, carry)
        return carry

    zero = jnp.zeros((rows, cols), f32)
    _, sum_u, sum_v, star_u, star_v = lax.fori_loop(
        0, half, momentum, (jnp.zeros((full, cols), f32), zero, zero, zero, zero))
    per_depth = thickness / jnp.maximum(thickness * count_here, thickness)
    sf[0, 0, SUB:top, :] = sum_u * per_depth
    sf[1, 0, SUB:top, :] = sum_v * per_depth
    mean_star_u = star_u * per_depth
    mean_star_v = star_v * per_depth
    force_lon_pair.start()

    def store(q, k0, k1, sem):
        part = pltpu.make_async_copy(out.at[q:q + 2, k0:k1], out_hbm.at[q:q + 2, k0:k1], store_sem.at[sem])
        part.start()
        return part

    stores = [store(2, 0, nlev, 0)]

    def tracers(i, carry):
        for slot in range(2):
            k = 2 * i + slot
            wet = (crow[SUB:top, :] > k.astype(f32)).astype(f32)
            s_lat = lat_speed(k, SUB, rows)
            for q in range(2):
                flux = face_rows(q, k, s_lat, SUB, rows)
                place = 2 * slot + q
                fbuf[place, SUB - 1:SUB, :] = extra_lat[q, pl.ds(k, 1), :]
                fbuf[place, SUB:top, :] = flux
                change = advect_lon(q, k, speed_lon[k]) + (flux - fbuf[place, SUB - 1:top - 1, :])
                out[q, k] = wet * (ext[q, k, SUB:top, :] - tracer_step * change)
        return carry

    mid = (3 * half) // 8
    lax.fori_loop(0, mid, tracers, 0)
    force_lon_pair.wait_recv()
    close_lon(sf, sf_lon, 2)
    stage_north(sf, sf_north, (-1.0, -1.0))
    force_lat_pair.start()
    stores.append(store(0, 0, 2 * mid, 1))
    lax.fori_loop(mid, half, tracers, 0)
    stores.append(store(0, 2 * mid, nlev, 2))
    surf_lat.wait_recv()
    force_lat_pair.wait_recv()

    def slope_lon(c, h):
        up_c = left(jnp.where(lane_full == 0, h, c), 1)
        up_h = left(jnp.where(lane_full == 0, c, h), 1)
        down_c = right(jnp.where(lane_full == cols - 1, h, c), 1)
        down_h = right(jnp.where(lane_full == cols - 1, c, h), 1)
        return 0.5 * (up_c - down_c), 0.5 * (up_h - down_h)

    def slope_lat(c, h):
        return tuple(0.5 * (pltpu.roll(a, full - 1, axis=0) - pltpu.roll(a, 1, axis=0)) for a in (c, h))

    both = (0, 1)
    height = [sa[0, i] for i in both]
    mean_u = [sa[1, i] for i in both]
    mean_v = [sa[2, i] for i in both]
    depth = [thickness * sa[3, i] for i in both]
    sea = [(sa[3, i] > 0.0).astype(f32) for i in both]
    for _ in range(NSUB):
        dx = slope_lon(*[depth[i] * mean_u[i] for i in both])
        dy = slope_lat(*[depth[i] * mean_v[i] for i in both])
        height = [sea[i] * (height[i] - surface_step * (dx[i] + dy[i])) for i in both]
        dx = slope_lon(*height)
        dy = slope_lat(*height)
        mean_u = [sea[i] * (mean_u[i] + surface_step * (sf[0, i] - dx[i])) for i in both]
        mean_v = [sea[i] * (mean_v[i] + surface_step * (sf[1, i] - dy[i])) for i in both]
    surf_out[0] = height[0][SUB:top]
    surf_out[1] = mean_u[0][SUB:top]
    surf_out[2] = mean_v[0][SUB:top]
    gain[0] = mean_u[0][SUB:top] - mean_star_u
    gain[1] = mean_v[0][SUB:top] - mean_star_v
    for part in stores:
        part.wait()

    for pair in (surf_lon, level_lon, level_lat, surf_lat, force_lon_pair, force_lat_pair):
        pair.wait_send()


def finish_kernel(stars, gain, surface, counts, out, surf_out, buf, gain_buf, surf_buf, count_buf, in_sem, out_sem):
    nlev = stars.shape[1]
    half = nlev // 2
    places = [(q, h) for q in (2, 3, 0, 1) for h in range(2)]
    copy = pltpu.make_async_copy
    small = [copy(gain, gain_buf, in_sem.at[8]), copy(counts, count_buf, in_sem.at[9]),
             copy(surface, surf_buf, in_sem.at[10])]
    loads = [copy(stars.at[q, h * half:(h + 1) * half], buf.at[q, h * half:(h + 1) * half], in_sem.at[i])
             for i, (q, h) in enumerate(places)]
    stores = [copy(buf.at[q, h * half:(h + 1) * half], out.at[q, h * half:(h + 1) * half], out_sem.at[i])
              for i, (q, h) in enumerate(places)]
    last = copy(surf_buf, surf_out, out_sem.at[8])
    for part in small + loads:
        part.start()
    for part in small:
        part.wait()
    last.start()
    for i, (q, h) in enumerate(places):
        loads[i].wait()
        if q >= 2:
            for k in range(h * half, (h + 1) * half):
                buf[q, k] = jnp.where(count_buf[...] > k, buf[q, k] + gain_buf[q - 2], 0.0)
        stores[i].start()
    for part in stores + [last]:
        part.wait()


def on_device(nx, ny, ocean_state, surface_state, column_levels):
    _, nlev, rows, cols = ocean_state.shape
    if cols % 128 or nlev * 8 > cols or nlev % 4 or rows % SUB or rows < 3 * SUB or DEEP > SUB or nx % 2:
        raise ValueError("tile shape")
    full = rows + 2 * SUB
    vmem = pltpu.VMEM
    stars, gain, surface_next = pl.pallas_call(
        functools.partial(kernel, nx, ny),
        out_shape=(jax.ShapeDtypeStruct(ocean_state.shape, f32), jax.ShapeDtypeStruct((2, rows, cols), f32),
                   jax.ShapeDtypeStruct(surface_state.shape, f32)),
        in_specs=[pl.BlockSpec(memory_space=pltpu.HBM)] * 3,
        out_specs=(pl.BlockSpec(memory_space=pl.ANY), pl.BlockSpec(memory_space=vmem), pl.BlockSpec(memory_space=vmem)),
        scratch_shapes=[
            vmem((4, nlev, full, cols), f32),
            vmem((4, rows, cols), f32),
            vmem((2, 4, rows, cols), f32),
            vmem((2, 2 * nlev + 1, SUB, cols), f32),
            vmem((2, 2 * nlev + 1, SUB, cols), f32),
            vmem((4, 2, full, cols), f32),
            vmem((2, 2, full, cols), f32),
            vmem((2, 4, rows, cols), f32),
            vmem((2, 2, rows, cols), f32),
            vmem((4, 2, SUB, cols), f32),
            vmem((2, 2, SUB, cols), f32),
            vmem((4, rows, cols), f32),
            vmem((4, nlev, cols), f32),
            vmem((nlev, rows, cols), f32),
            vmem((2, full, cols), f32),
            vmem((4, full, cols), f32),
            vmem((2, nlev, rows - 2 * SUB, cols), f32),
            vmem((4, nlev, rows, cols), f32),
            vmem((rows, cols), jnp.int32),
            vmem((full, cols), f32),
            vmem((5, rows, cols), f32),
            pltpu.SemaphoreType.DMA((3,)),
            pltpu.SemaphoreType.DMA((3,)),
            pltpu.SemaphoreType.DMA((12,)),
            pltpu.SemaphoreType.DMA((12,)),
        ],
        compiler_params=pltpu.CompilerParams(collective_id=0, has_side_effects=True),
    )(ocean_state, surface_state, column_levels)
    parts = 8
    return pl.pallas_call(
        finish_kernel,
        out_shape=(jax.ShapeDtypeStruct(ocean_state.shape, f32), jax.ShapeDtypeStruct(surface_state.shape, f32)),
        in_specs=[pl.BlockSpec(memory_space=pl.ANY)] * 4,
        out_specs=(pl.BlockSpec(memory_space=pl.ANY),) * 2,
        scratch_shapes=[
            vmem(ocean_state.shape, f32),
            vmem((2, rows, cols), f32),
            vmem(surface_state.shape, f32),
            vmem((rows, cols), jnp.int32),
            pltpu.SemaphoreType.DMA((parts + 3,)),
            pltpu.SemaphoreType.DMA((parts + 1,)),
        ],
    )(stars, gain, surface_next, column_levels)


def solution(mesh):
    return jax.shard_map(
        functools.partial(on_device, mesh.shape["lon"], mesh.shape["lat"]),
        mesh=mesh,
        in_specs=(P(None, None, "lat", "lon"), P(None, "lat", "lon"), P("lat", "lon")),
        out_specs=(P(None, None, "lat", "lon"), P(None, "lat", "lon")),
        check_vma=False,
    )
```

```python
import functools
import math

import jax
import jax.numpy as jnp
from jax import lax
from jax.experimental import pallas as pl
from jax.experimental.pallas import tpu as pltpu
from jax.sharding import PartitionSpec as P

NSUB = 4
DEEP = 2 * NSUB
SUB = 8
epsilon = 1e-06
tracer_step = 0.1
surface_step = 1.2
f32 = jnp.float32


def face_flux(s, q0, q1, dm2, dm1, d0, dp1, dp2):
    pos = s >= 0.0
    third = jnp.abs(s) * (1.0 / 3.0)
    c = jnp.where(pos, q0, q1)
    d1 = jnp.where(pos, dm2, dp2)
    d2 = jnp.where(pos, dm1, dp1)
    d3 = d0
    d4 = jnp.where(pos, dp1, dm1)
    rest2 = ((39.0 / 64.0) * d2) * d2 + 0.75 * epsilon
    rest3 = ((39.0 / 64.0) * d3) * d3 + 0.75 * epsilon
    g1 = d1 - (11.0 / 8.0) * d2
    g2 = d2 - (5.0 / 8.0) * d3
    g3 = d4 - (11.0 / 8.0) * d3
    s1 = g1 * g1 + rest2
    s2 = g2 * g2 + rest3
    s3 = g3 * g3 + rest3
    p23 = s2 * s3
    p13 = s1 * s3
    p12 = s1 * s2
    w1 = (p23 * (1.0 / 3.0)) * p23
    w2 = p13 * p13
    w3 = p12 * p12
    twice = d3 + d3
    top = w1 * (2.5 * d2 - d1) + w2 * (d2 + twice) + w3 * (twice - 0.5 * d4)
    total = (w1 + w2) + (w2 + w3)
    return s * c + third * (top * pl.reciprocal(total, approx=True))


def left(x, n):
    return pltpu.roll(x, x.shape[-1] - n, axis=x.ndim - 1)


def right(x, n):
    return pltpu.roll(x, n, axis=x.ndim - 1)


def kernel(nx, ny, ocean, surface, levels_in, out_hbm, gain, surf_out, ext, lon_own, lon_in, lat_out, lat_in, sa, sf,
           sa_lon, sf_lon, sa_north, sf_north, extra_lon, extra_lat, speed_lon, pbuf, fbuf,
           flat, out, counts, crow, lon_both, local_sem, store_sem, send_sem, recv_sem):
    nlev, rows, cols = ocean.shape[1], ocean.shape[2], ocean.shape[3]
    top = SUB + rows
    full = top + SUB
    thickness = 1.0 / nlev
    wide = 8
    x = lax.axis_index("lon")
    y = lax.axis_index("lat")
    at_north = y == ny - 1
    east = {"lon": lax.rem(x + 1, nx), "lat": y}
    west = {"lon": lax.rem(x + nx - 1, nx), "lat": y}
    north = {"lon": jnp.where(at_north, nx - 1 - x, x), "lat": jnp.where(at_north, y, y + 1)}
    south = {"lon": x, "lat": jnp.maximum(y - 1, 0)}
    fold = jnp.where(at_north, 1, 0)
    far_row = pl.multiple_of(fold * top, SUB)

    load = pltpu.make_async_copy(ocean, ext.at[:, :, SUB:top, :], local_sem.at[0])
    load_surface = pltpu.make_async_copy(surface, sa.at[0:3, 0, SUB:top, :], local_sem.at[1])
    load_counts = pltpu.make_async_copy(levels_in, counts, local_sem.at[2])
    load.start()
    load_surface.start()
    load_counts.start()

    @pl.when(y == 0)
    def _():
        sa[:, :, 0:SUB, :] = jnp.zeros((4, 2, SUB, cols), f32)
        sf[:, :, 0:SUB, :] = jnp.zeros((2, 2, SUB, cols), f32)
        lat_in[0] = jnp.zeros(lat_in.shape[1:], f32)

    barrier = pltpu.get_barrier_semaphore()
    for target in (east, west, north):
        pl.semaphore_signal(barrier, inc=1, device_id=target, device_id_type=pl.DeviceIdType.MESH)

    @pl.when(y > 0)
    def _():
        pl.semaphore_signal(barrier, inc=1, device_id=south, device_id_type=pl.DeviceIdType.MESH)

    def remote(src, dst, send, recv, target):
        return pltpu.make_async_remote_copy(
            src_ref=src, dst_ref=dst, send_sem=send_sem.at[send], recv_sem=recv_sem.at[recv],
            device_id=target, device_id_type=pl.DeviceIdType.MESH)

    class LonPair:
        def __init__(self, src, dst, base):
            self.go_east = remote(src, dst.at[0], base, base, east)
            self.go_west = remote(src, dst.at[1], base + 1, base + 1, west)

        def start(self):
            self.go_east.start()
            self.go_west.start()

        def wait_recv(self):
            self.go_east.wait_recv()
            self.go_west.wait_recv()

        def wait_send(self):
            self.go_east.wait_send()
            self.go_west.wait_send()

    class LatPair:
        def __init__(self, north_src, north_dst, south_src, dst_south, dst_north, base):
            self.go_north = remote(north_src, north_dst, base, base + fold, north)
            self.go_south = remote(south_src, dst_north, base + 1, base + 1, south)
            self.from_south = remote(north_src, dst_south, base, base, south)

        def start(self):
            self.go_north.start()

            @pl.when(y > 0)
            def _():
                self.go_south.start()

        def wait_recv(self):
            self.go_south.wait_recv()

            @pl.when(y > 0)
            def _():
                self.from_south.wait_recv()

        def wait_send(self):
            self.go_north.wait_send()

            @pl.when(y > 0)
            def _():
                self.go_south.wait_send()

    surf_lon = LonPair(sa.at[:, 0, SUB:top, :], sa_lon, 0)
    level_lon = LonPair(lon_own, lon_in, 2)
    force_lon_pair = LonPair(sf.at[:, 0, SUB:top, :], sf_lon, 4)
    level_lat = LatPair(lat_out.at[0], lat_in.at[fold], lat_out.at[1], lat_in.at[0], lat_in.at[1], 6)
    surf_lat = LatPair(sa_north, sa.at[:, :, pl.ds(far_row, SUB), :], sa.at[:, :, SUB:2 * SUB, :],
                       sa.at[:, :, 0:SUB, :], sa.at[:, :, top:full, :], 8)
    force_lat_pair = LatPair(sf_north, sf.at[:, :, pl.ds(far_row, SUB), :], sf.at[:, :, SUB:2 * SUB, :],
                             sf.at[:, :, 0:SUB, :], sf.at[:, :, top:full, :], 10)

    lane = lax.broadcasted_iota(jnp.int32, (rows, cols), 1)
    lane_full = lax.broadcasted_iota(jnp.int32, (full, cols), 1)
    spot = lane % wide
    owner = lane // wide
    sub8 = lax.broadcasted_iota(jnp.int32, (SUB, cols), 0)

    def mirrored(tiles):
        for axis, length in ((1, SUB), (2, cols)):
            at = lax.broadcasted_iota(jnp.int32, tiles.shape, axis)
            step = 1
            while step < length:
                turned = pltpu.roll(tiles, step, axis=axis)
                if 2 * step < length:
                    turned = jnp.where((at // step) % 2 == 1, turned, pltpu.roll(tiles, length - step, axis=axis))
                tiles = turned
                step *= 2
        return tiles

    load.wait()
    half = nlev // 2
    for q in range(4):
        for h in range(half):
            n0 = ext[q, 2 * h, top - SUB:top, :]
            n1 = ext[q, 2 * h + 1, top - SUB:top, :]
            lat_out[0, q * half + h] = jnp.where(sub8 >= 4, n0, pltpu.roll(n1, 4, axis=0))
            s0 = ext[q, 2 * h, SUB:2 * SUB, :]
            s1 = ext[q, 2 * h + 1, SUB:2 * SUB, :]
            lat_out[1, q * half + h] = jnp.where(sub8 < 4, s0, pltpu.roll(s1, 4, axis=0))

    load_surface.wait()
    load_counts.wait()
    sa[3, 0, SUB:top, :] = counts[...].astype(f32)
    crow[SUB:top, :] = sa[3, 0, SUB:top, :]
    lat_out[0, 4 * half] = crow[top - SUB:top, :]
    lat_out[1, 4 * half] = crow[SUB:2 * SUB, :]

    @pl.when(at_north)
    def _():
        lat_out[0] = mirrored(jnp.concatenate(
            [lat_out[0, 0:2 * half], -lat_out[0, 2 * half:4 * half], lat_out[0, 4 * half:]], axis=0))

    pl.semaphore_wait(barrier, 3 + jnp.where(y > 0, 1, 0))
    level_lat.start()
    surf_lon.start()

    for q in range(4):
        pack = jnp.zeros((rows, cols), f32)
        for k in range(nlev):
            pack = jnp.where(owner == k, right(ext[q, k, SUB:top, :], wide * k + 3), pack)
        lon_own[q] = pack
    level_lon.start()

    def close_lon(fields, arrived, count):
        for f in range(count):
            fields[f, 1, SUB:top, :] = jnp.where(lane < cols // 2, arrived[1, f], arrived[0, f])

    def stage_north(fields, staged, signs):
        count = len(signs)
        for f in range(count):
            for part in range(2):
                staged[f, part] = fields[f, part, top - SUB:top, :]

        @pl.when(at_north)
        def _():
            staged[...] = mirrored(jnp.concatenate(
                [signs[f] * staged[f] for f in range(count)], axis=0)).reshape(count, 2, SUB, cols)

    def face_rows(q, k, s, first, count):
        start = first - 2 + jnp.minimum(k, 0)
        cell = [ext[q, k, pl.ds(start + i, count), :] for i in range(6)]
        return face_flux(s, cell[2], cell[3], *[cell[i + 1] - cell[i] for i in range(5)])

    def lat_speed(k, first, count):
        least = jnp.minimum(crow[first:first + count, :], crow[first + 1:first + 1 + count, :])
        speed = 0.5 * (ext[3, k, first:first + count, :] + ext[3, k, first + 1:first + 1 + count, :])
        return jnp.where(least > k.astype(f32), speed, 0.0)

    inner, inner_count = 2 * SUB, rows - 2 * SUB

    def inner_faces(i, carry):
        for k in (2 * i, 2 * i + 1):
            s = lat_speed(k, inner, inner_count)
            for q in (2, 3):
                flat[q - 2, k] = face_rows(q, k, s, inner, inner_count)
        return carry

    lax.fori_loop(0, half, inner_faces, 0)

    surf_lon.wait_recv()
    close_lon(sa, sa_lon, 4)
    stage_north(sa, sa_north, (1.0, -1.0, -1.0, 1.0))
    surf_lat.start()

    level_lon.wait_recv()

    def lon_pack(q):
        return jnp.where(spot < 3, lon_in[0, q], lon_own[q])

    count_here = crow[SUB:top, :]
    count_beside = sa[3, 1, SUB:top, :]
    level_of = owner.astype(f32)
    for q in range(4):
        lon_both[q] = jnp.where(spot < 3, lon_in[0, q], lon_in[1, q])
    edge_wet = ((count_beside[:, cols - 1:cols] > level_of) & (count_here[:, 0:1] > level_of)).astype(f32)
    pack_u = lon_pack(2)
    edge_speed = 0.5 * (pack_u + left(pack_u, 1)) * edge_wet
    for q in range(4):
        pack = lon_pack(q)
        d = left(pack, 1) - pack
        extra_lon[q] = face_flux(edge_speed, pack, left(pack, 1), right(d, 2), right(d, 1), d, left(d, 1),
                                 left(d, 2))

    def beside(q, k):
        return pltpu.roll(lon_both[q], cols - 3 - wide * k, axis=1)

    def following(c, h):
        return left(jnp.where(lane == 0, h, c), 1)

    def advect_lon(q, k, s_lon):
        c = ext[q, k, SUB:top, :]
        h = beside(q, k)
        c1 = following(c, h)
        d = c1 - c
        dh = following(h, c) - h
        flux = face_flux(
            s_lon, c, c1,
            right(jnp.where(lane >= cols - 2, dh, d), 2),
            right(jnp.where(lane >= cols - 1, dh, d), 1),
            d,
            left(jnp.where(lane < 1, dh, d), 1),
            left(jnp.where(lane < 2, dh, d), 2))
        edge = pltpu.roll(extra_lon[q], cols - 2 - wide * k, axis=1)
        return flux - jnp.where(lane == 0, edge, right(flux, 1))

    least_lon = jnp.minimum(count_here, following(count_here, count_beside))

    level_lat.wait_recv()
    crow[0:SUB, :] = lat_in[0, 4 * half]
    crow[top:full, :] = lat_in[1, 4 * half]

    for q in range(4):
        for h in range(half):
            for side, place in ((0, 0), (1, top)):
                block = lat_in[side, q * half + h]
                ext[q, 2 * h, place:place + SUB, :] = block
                ext[q, 2 * h + 1, place:place + SUB, :] = pltpu.roll(block, 4, axis=0)

    level_row = lax.broadcasted_iota(jnp.int32, (nlev, cols), 0).astype(f32)
    row_wet = ((crow[SUB - 1:SUB, :] > level_row) & (crow[SUB:SUB + 1, :] > level_row)).astype(f32)
    row_speed = 0.5 * (ext[3, :, SUB - 1, :] + ext[3, :, SUB, :]) * row_wet
    for q in range(4):
        cell = [ext[q, :, SUB - 3 + i, :] for i in range(6)]
        d = [cell[i + 1] - cell[i] for i in range(5)]
        extra_lat[q] = face_flux(row_speed, cell[2], cell[3], *d)

    def advect_lat(q, k, s_south, s_north, slot):
        fbuf[slot, SUB - 1:SUB, :] = extra_lat[q, pl.ds(k, 1), :]
        fbuf[slot, SUB:2 * SUB, :] = face_rows(q, k, s_south, SUB, SUB)
        fbuf[slot, inner:top - SUB, :] = flat[q - 2, k]
        fbuf[slot, top - SUB:top, :] = face_rows(q, k, s_north, top - SUB, SUB)
        return fbuf[slot, SUB:top, :] - fbuf[slot, SUB - 1:top - 1, :]

    row = lax.broadcasted_iota(jnp.int32, (rows, cols), 0)
    latitude = ((y * rows + row).astype(f32) + 0.5) / float(ny * rows)
    coriolis = jnp.sin(math.pi * latitude - 0.5 * math.pi)

    def density(t, s, wet):
        return wet * (-0.2 * t + 0.8 * s - 0.05 * t * t + 0.03 * t * s)

    beside_wet = jnp.where(spot < 3, count_beside[:, cols - 1:cols], count_beside[:, 0:1]) > level_of
    rho_beside = density(lon_both[0], lon_both[1], beside_wet.astype(f32))
    total_beside = rho_beside
    step = 1
    while step < nlev:
        total_beside = total_beside + jnp.where(owner >= step, right(total_beside, wide * step), 0.0)
        step *= 2
    lon_both[4] = thickness * (total_beside - 0.5 * rho_beside)
    def momentum_level(k, slot, carry):
        above, sum_u, sum_v, star_u, star_v = carry
        level = k.astype(f32)
        wet_full = (crow[...] > level).astype(f32)
        wet = (crow[SUB:top, :] > level).astype(f32)
        rho = density(ext[0, k], ext[1, k], wet_full)
        above = above + rho
        pressure = thickness * (above - 0.5 * rho)
        pressure_h = beside(4, k)
        pbuf[slot] = pressure
        p = pbuf[slot, SUB:top, :]
        grad_lon = 0.5 * (following(p, pressure_h) - right(jnp.where(lane == cols - 1, pressure_h, p), 1))
        grad_lat = 0.5 * (pbuf[slot, SUB + 1:top + 1, :] - pbuf[slot, SUB - 1:top - 1, :])
        u = ext[2, k, SUB:top, :]
        v = ext[3, k, SUB:top, :]
        s_lon = jnp.where(least_lon > level, 0.5 * (u + following(u, beside(2, k))), 0.0)
        speed_lon[k] = s_lon
        s_south = lat_speed(k, SUB, SUB)
        s_north = lat_speed(k, top - SUB, SUB)
        accel_u = wet * (coriolis * v - (advect_lon(2, k, s_lon) + advect_lat(2, k, s_south, s_north, 2 * slot)) - grad_lon)
        accel_v = wet * (-(advect_lon(3, k, s_lon) + advect_lat(3, k, s_south, s_north, 2 * slot + 1)) - coriolis * u - grad_lat)
        u_star = wet * u + tracer_step * accel_u
        v_star = wet * v + tracer_step * accel_v
        out[2, k] = u_star
        out[3, k] = v_star
        return above, sum_u + accel_u, sum_v + accel_v, star_u + u_star, star_v + v_star

    def momentum(i, carry):
        for slot in range(2):
            carry = momentum_level(2 * i + slot, slot, carry)
        return carry

    zero = jnp.zeros((rows, cols), f32)
    _, sum_u, sum_v, star_u, star_v = lax.fori_loop(
        0, half, momentum, (jnp.zeros((full, cols), f32), zero, zero, zero, zero))
    per_depth = thickness / jnp.maximum(thickness * count_here, thickness)
    sf[0, 0, SUB:top, :] = sum_u * per_depth
    sf[1, 0, SUB:top, :] = sum_v * per_depth
    mean_star_u = star_u * per_depth
    mean_star_v = star_v * per_depth
    force_lon_pair.start()

    def store(q, k0, k1, sem):
        part = pltpu.make_async_copy(out.at[q:q + 2, k0:k1], out_hbm.at[q:q + 2, k0:k1], store_sem.at[sem])
        part.start()
        return part

    stores = [store(2, 0, nlev, 0)]

    def tracers(i, carry):
        for slot in range(2):
            k = 2 * i + slot
            wet = (crow[SUB:top, :] > k.astype(f32)).astype(f32)
            s_lat = lat_speed(k, SUB, rows)
            for q in range(2):
                flux = face_rows(q, k, s_lat, SUB, rows)
                place = 2 * slot + q
                fbuf[place, SUB - 1:SUB, :] = extra_lat[q, pl.ds(k, 1), :]
                fbuf[place, SUB:top, :] = flux
                change = advect_lon(q, k, speed_lon[k]) + (flux - fbuf[place, SUB - 1:top - 1, :])
                out[q, k] = wet * (ext[q, k, SUB:top, :] - tracer_step * change)
        return carry

    mid = (3 * half) // 8
    lax.fori_loop(0, mid, tracers, 0)
    force_lon_pair.wait_recv()
    close_lon(sf, sf_lon, 2)
    stage_north(sf, sf_north, (-1.0, -1.0))
    force_lat_pair.start()
    stores.append(store(0, 0, 2 * mid, 1))
    lax.fori_loop(mid, half, tracers, 0)
    stores.append(store(0, 2 * mid, nlev, 2))
    surf_lat.wait_recv()

    def slope_lon(c, h):
        up_c = left(jnp.where(lane_full == 0, h, c), 1)
        up_h = left(jnp.where(lane_full == 0, c, h), 1)
        down_c = right(jnp.where(lane_full == cols - 1, h, c), 1)
        down_h = right(jnp.where(lane_full == cols - 1, c, h), 1)
        return 0.5 * (up_c - down_c), 0.5 * (up_h - down_h)

    def slope_lat(c, h):
        return tuple(0.5 * (pltpu.roll(a, full - 1, axis=0) - pltpu.roll(a, 1, axis=0)) for a in (c, h))

    both = (0, 1)
    height = [sa[0, i] for i in both]
    mean_u = [sa[1, i] for i in both]
    mean_v = [sa[2, i] for i in both]
    depth = [thickness * sa[3, i] for i in both]
    sea = [(sa[3, i] > 0.0).astype(f32) for i in both]
    for substep in range(NSUB):
        dx = slope_lon(*[depth[i] * mean_u[i] for i in both])
        dy = slope_lat(*[depth[i] * mean_v[i] for i in both])
        height = [sea[i] * (height[i] - surface_step * (dx[i] + dy[i])) for i in both]
        dx = slope_lon(*height)
        dy = slope_lat(*height)
        if substep == 0:
            force_lat_pair.wait_recv()
        mean_u = [sea[i] * (mean_u[i] + surface_step * (sf[0, i] - dx[i])) for i in both]
        mean_v = [sea[i] * (mean_v[i] + surface_step * (sf[1, i] - dy[i])) for i in both]
    surf_out[0] = height[0][SUB:top]
    surf_out[1] = mean_u[0][SUB:top]
    surf_out[2] = mean_v[0][SUB:top]
    gain[0] = mean_u[0][SUB:top] - mean_star_u
    gain[1] = mean_v[0][SUB:top] - mean_star_v
    for part in stores:
        part.wait()

    for pair in (surf_lon, level_lon, level_lat, surf_lat, force_lon_pair, force_lat_pair):
        pair.wait_send()


def finish_kernel(stars, gain, surface, counts, out, surf_out, buf, gain_buf, surf_buf, count_buf, in_sem, out_sem):
    nlev = stars.shape[1]
    half = nlev // 2
    places = [(q, h) for q in (2, 3, 0, 1) for h in range(2)]
    copy = pltpu.make_async_copy
    small = [copy(gain, gain_buf, in_sem.at[8]), copy(counts, count_buf, in_sem.at[9]),
             copy(surface, surf_buf, in_sem.at[10])]
    loads = [copy(stars.at[q, h * half:(h + 1) * half], buf.at[q, h * half:(h + 1) * half], in_sem.at[i])
             for i, (q, h) in enumerate(places)]
    stores = [copy(buf.at[q, h * half:(h + 1) * half], out.at[q, h * half:(h + 1) * half], out_sem.at[i])
              for i, (q, h) in enumerate(places)]
    last = copy(surf_buf, surf_out, out_sem.at[8])
    for part in small + loads:
        part.start()
    for part in small:
        part.wait()
    last.start()
    for i, (q, h) in enumerate(places):
        loads[i].wait()
        if q >= 2:
            for k in range(h * half, (h + 1) * half):
                buf[q, k] = jnp.where(count_buf[...] > k, buf[q, k] + gain_buf[q - 2], 0.0)
        stores[i].start()
    for part in stores + [last]:
        part.wait()


def on_device(nx, ny, ocean_state, surface_state, column_levels):
    _, nlev, rows, cols = ocean_state.shape
    if cols % 128 or nlev * 8 > cols or nlev % 4 or rows % SUB or rows < 3 * SUB or DEEP > SUB or nx % 2:
        raise ValueError("tile shape")
    full = rows + 2 * SUB
    vmem = pltpu.VMEM
    stars, gain, surface_next = pl.pallas_call(
        functools.partial(kernel, nx, ny),
        out_shape=(jax.ShapeDtypeStruct(ocean_state.shape, f32), jax.ShapeDtypeStruct((2, rows, cols), f32),
                   jax.ShapeDtypeStruct(surface_state.shape, f32)),
        in_specs=[pl.BlockSpec(memory_space=pltpu.HBM)] * 3,
        out_specs=(pl.BlockSpec(memory_space=pl.ANY), pl.BlockSpec(memory_space=vmem), pl.BlockSpec(memory_space=vmem)),
        scratch_shapes=[
            vmem((4, nlev, full, cols), f32),
            vmem((4, rows, cols), f32),
            vmem((2, 4, rows, cols), f32),
            vmem((2, 2 * nlev + 1, SUB, cols), f32),
            vmem((2, 2 * nlev + 1, SUB, cols), f32),
            vmem((4, 2, full, cols), f32),
            vmem((2, 2, full, cols), f32),
            vmem((2, 4, rows, cols), f32),
            vmem((2, 2, rows, cols), f32),
            vmem((4, 2, SUB, cols), f32),
            vmem((2, 2, SUB, cols), f32),
            vmem((4, rows, cols), f32),
            vmem((4, nlev, cols), f32),
            vmem((nlev, rows, cols), f32),
            vmem((2, full, cols), f32),
            vmem((4, full, cols), f32),
            vmem((2, nlev, rows - 2 * SUB, cols), f32),
            vmem((4, nlev, rows, cols), f32),
            vmem((rows, cols), jnp.int32),
            vmem((full, cols), f32),
            vmem((5, rows, cols), f32),
            pltpu.SemaphoreType.DMA((3,)),
            pltpu.SemaphoreType.DMA((3,)),
            pltpu.SemaphoreType.DMA((12,)),
            pltpu.SemaphoreType.DMA((12,)),
        ],
        compiler_params=pltpu.CompilerParams(collective_id=0, has_side_effects=True),
    )(ocean_state, surface_state, column_levels)
    parts = 8
    return pl.pallas_call(
        finish_kernel,
        out_shape=(jax.ShapeDtypeStruct(ocean_state.shape, f32), jax.ShapeDtypeStruct(surface_state.shape, f32)),
        in_specs=[pl.BlockSpec(memory_space=pl.ANY)] * 4,
        out_specs=(pl.BlockSpec(memory_space=pl.ANY),) * 2,
        scratch_shapes=[
            vmem(ocean_state.shape, f32),
            vmem((2, rows, cols), f32),
            vmem(surface_state.shape, f32),
            vmem((rows, cols), jnp.int32),
            pltpu.SemaphoreType.DMA((parts + 3,)),
            pltpu.SemaphoreType.DMA((parts + 1,)),
        ],
    )(stars, gain, surface_next, column_levels)


def solution(mesh):
    return jax.shard_map(
        functools.partial(on_device, mesh.shape["lon"], mesh.shape["lat"]),
        mesh=mesh,
        in_specs=(P(None, None, "lat", "lon"), P(None, "lat", "lon"), P("lat", "lon")),
        out_specs=(P(None, None, "lat", "lon"), P(None, "lat", "lon")),
        check_vma=False,
    )
```
